128 devices in a mesh: dp: 2 (over z_hi), blk: 8 (over z_lo, y), uly: 8 (over x, core).
Axes of the slice: x: 4, y: 4, z: 4 (z_hi: 2, z_lo: 2; z = z_hi * 2 + z_lo), core: 2. Of those that a mesh axis runs over, the one named last changes fastest.
Arguments:
- query_rows: bfloat16 [8192, 3072], P(('dp', 'blk', 'uly')), may hold values from -76 to 76
- key_rows: bfloat16 [8192, 3072], P(('dp', 'blk', 'uly')), may hold values from -8 to 8
- value_rows: bfloat16 [8192, 3072], P(('dp', 'blk', 'uly')), may hold values from -6 to 6
- out_grad: bfloat16 [8192, 5120], P(('dp', 'blk', 'uly')), may hold values from -24 to 24
- out_weight: bfloat16 [5120, 3072], P(('dp', 'blk'), 'uly'), may hold values from -2.5 to 2.5
Outputs:
- grad_query: bfloat16 [8192, 3072], P(('dp', 'blk', 'uly'))
- grad_key: bfloat16 [8192, 3072], P(('dp', 'blk', 'uly'))
- grad_value: bfloat16 [8192, 3072], P(('dp', 'blk', 'uly'))
- grad_weight: float32 [5120, 3072], P(('dp', 'blk'), 'uly')
The draws below stay inside these ranges and needn't reach their ends.
All inputs are finite; a program needn't handle non-finite values.
Results may differ from the reference program's by a relative error of at most 0.0059.
Values may be sent and summed in bfloat16 or wider, within the bound.
No kernel may reach another device: no remote copies, remote signals or barrier semaphores. Data moves between devices by JAX's collectives and lax.ppermute only.
A program may use at most 128 MiB of HBM per device.

```python
import jax
import jax.numpy as jnp
from jax import lax

HEADS = 24
HD = 128
D = 5120
SEQ = 4096
TOKENS = 8192
N_DP = 2
N_BLK = 8


def shared_keys(key):
    normal_keys = jax.random.normal(jax.random.fold_in(key, 5), (TOKENS, HEADS * HD), jnp.float32)
    return jnp.clip(normal_keys, -4.5, 4.5)


def distant_partners(base_rows, key):
    block_key = jax.random.fold_in(key, 41)
    spot_key = jax.random.fold_in(key, 43)
    pull_key = jax.random.fold_in(key, 47)
    block_size = SEQ // N_BLK
    head_blocks = jax.random.randint(block_key, (1, HEADS), 1, N_BLK)
    spots = jax.random.randint(spot_key, (TOKENS, HEADS), 0, block_size)
    rows = jnp.arange(TOKENS, dtype=jnp.int32)[:, None]
    clip_start = rows // SEQ * SEQ
    target = clip_start + (rows - clip_start + head_blocks * block_size + spots) % SEQ
    head_index = jnp.arange(HEADS, dtype=jnp.int32)[None, :]
    stacked = base_rows.reshape(TOKENS, HEADS, HD)
    partners = stacked[target, head_index]
    pull = jax.random.uniform(pull_key, (TOKENS, HEADS, 1), jnp.float32, 0.6, 1.0)
    return (pull * partners).reshape(TOKENS, HEADS * HD)


def draw_key_rows(key, part):
    base_rows = shared_keys(key)
    return base_rows.astype(jnp.bfloat16)


def draw_query_rows(key, part):
    base_rows = shared_keys(key)
    key = jax.random.fold_in(key, 37)
    drawn = jnp.clip(jax.random.normal(key, (TOKENS, HEADS * HD), jnp.float32), -4.5, 4.5)
    drawn = drawn + distant_partners(base_rows, key)
    return drawn.astype(jnp.bfloat16)


def strengthened(values, own_key, source, target, shards_of, factor):
    owner, partner = [(jnp.arange(values.shape[dim]) // (values.shape[dim] // shards_of)).reshape([-1 if axis == dim else 1 for axis in range(values.ndim)]) for dim in (source, target)]
    chosen = jax.random.permutation(own_key, shards_of)[partner]
    strong = (owner == chosen) | (owner == (partner + shards_of // 2) % shards_of)
    return jnp.where(strong, factor * values, values)


def shard_levels(stream_key, dims, pieces, smallest, largest):
    def one(axis_at, blocks):
        draws = jax.random.uniform(jax.random.fold_in(jax.random.fold_in(stream_key, 6), axis_at), (blocks,), jnp.float32, smallest / len(pieces), largest / len(pieces))
        return jnp.repeat(jnp.exp(draws), dims[axis_at] // blocks).reshape((-1,) + (1,) * (len(dims) - axis_at - 1))

    gain = one(*pieces[0])
    for cut in pieces[1:]:
        gain = gain * one(*cut)
    return gain


def centred(key, dims, spread, limit, pieces=(), kind=jnp.bfloat16):
    values = jax.random.normal(key, dims, jnp.float32) * spread
    if len(pieces) > 0:
        values = shard_levels(key, dims, pieces, -0.22, 0.18) * values
    return jnp.clip(values, min=-limit, max=limit).astype(kind)


def noise_with(rng, shape, width, bound, split, heavy, held_as=jnp.bfloat16):
    values = width * jax.random.normal(rng, shape, jnp.float32)
    if split:
        values = values * shard_levels(rng, shape, split, -0.22, 0.18)
    return jnp.clip(strengthened(values, jax.random.fold_in(rng, 3), *heavy), -bound, bound).astype(held_as)


def setup_inputs(seed: int = 0) -> dict:
    key_of = jax.random.split(jax.random.key(seed), 6)
    return {
        "query_rows": draw_query_rows(jax.random.fold_in(key_of[5], 71), 0),
        "key_rows": draw_key_rows(jax.random.fold_in(key_of[5], 71), 0),
        "value_rows": centred(key_of[2], (TOKENS, HEADS * HD), 1.0, 6.0, ((0, 128),)),
        "out_grad": noise_with(key_of[3], (TOKENS, D), 1.0, 24.0, ((0, 128),), (0, 1, 128, 5.5)),
        "out_weight": centred(key_of[4], (D, HEADS * HD), 0.2, 2.5, ((0, 16), (1, 8))),
    }


def head_grads(queries, keys, values, grad_out):
    score_scale = HD ** -0.5
    scores = jnp.dot(queries, keys.T, preferred_element_type=jnp.float32) * score_scale
    log_total = jax.nn.logsumexp(scores, axis=1)
    probs_full = jnp.exp(scores - log_total[:, None])
    attn_out = jnp.dot(probs_full, values.astype(jnp.float32), precision=lax.Precision.HIGHEST)
    row_dot = jnp.sum(grad_out.astype(jnp.float32) * attn_out, axis=1)
    grad_probs = jnp.dot(grad_out, values.T, preferred_element_type=jnp.float32)
    grad_scores = (probs_full * (grad_probs - row_dot[:, None])).astype(jnp.bfloat16)
    probs_low = probs_full.astype(jnp.bfloat16)
    grad_values = jnp.dot(probs_low.T, grad_out, preferred_element_type=jnp.float32).astype(jnp.bfloat16)
    grad_keys = (jnp.dot(grad_scores.T, queries, preferred_element_type=jnp.float32) * score_scale).astype(jnp.bfloat16)
    grad_queries = (jnp.dot(grad_scores, keys, preferred_element_type=jnp.float32) * score_scale).astype(jnp.bfloat16)
    return grad_queries, grad_keys, grad_values, attn_out


def to_heads(matrix):
    return matrix.reshape(N_DP, SEQ, HEADS, HD).transpose(0, 2, 1, 3).reshape(N_DP * HEADS, SEQ, HD)


def to_tokens(stacked):
    return stacked.reshape(N_DP, HEADS, SEQ, HD).transpose(0, 2, 1, 3).reshape(N_DP * SEQ, HEADS * HD)


def reference(query_rows, key_rows, value_rows, out_grad, out_weight):
    grad_attn = jnp.dot(out_grad, out_weight, preferred_element_type=jnp.float32).astype(jnp.bfloat16)

    def one_head(bundle):
        return head_grads(bundle[0], bundle[1], bundle[2], bundle[3])

    grad_q, grad_k, grad_v, attn_heads = lax.map(one_head, (to_heads(query_rows), to_heads(key_rows), to_heads(value_rows), to_heads(grad_attn)))
    attn_out = to_tokens(attn_heads)
    grad_weight = lax.dot_general(out_grad.astype(jnp.float32), attn_out, (((0,), (0,)), ((), ())), precision=lax.Precision.HIGHEST)
    return to_tokens(grad_q), to_tokens(grad_k), to_tokens(grad_v), grad_weight
```

```python
import functools

import jax
import jax.numpy as jnp
from jax import lax
from jax.experimental import pallas as pl
from jax.experimental.pallas import tpu as pltpu
from jax.sharding import PartitionSpec as P

HD = 128
HEADS = 3
U = 8
T = 64
W = HEADS * HD
ROWS = U * T
SCALE = HD**-0.5
SCALE2 = SCALE * 1.4426950408889634
BF = jnp.bfloat16
F32 = jnp.float32
VMEM = 48 * 1024 * 1024


def nt(a, b):
    return lax.dot_general(a, b, (((1,), (1,)), ((), ())), preferred_element_type=F32)


def nn(a, b):
    return jnp.dot(a, b, preferred_element_type=F32)


def flat(ref):
    return ref[...].reshape(ROWS, HD)


def forward_kernel(qa, qb, kv0, kv1, kv2, k3, v3, ot_ref, st_ref):
    keys = jnp.concatenate(
        [kv0[:, 0].reshape(ROWS, HD), kv1[:, 0].reshape(ROWS, HD), kv2[:, 0].reshape(ROWS, HD), flat(k3)], axis=0
    )
    values = jnp.concatenate(
        [kv0[:, 1].reshape(ROWS, HD), kv1[:, 1].reshape(ROWS, HD), kv2[:, 1].reshape(ROWS, HD), flat(v3)], axis=0
    )
    values_t = values.T
    for part, q in enumerate((qa, qb)):
        queries = flat(q)
        for tile in range(2):
            at = part * ROWS + tile * 256
            scores = nt(keys, queries[tile * 256 : (tile + 1) * 256])
            top = jnp.max(scores, axis=0, keepdims=True) * SCALE2
            weights = jnp.exp2(scores * SCALE2 - top)
            total = jnp.sum(weights, axis=0, keepdims=True)
            ot_ref[:, at : at + 256] = nn(values_t, weights.astype(BF))
            st_ref[0, 0:1, at : at + 256] = top
            st_ref[0, 1:2, at : at + 256] = total


def head_block(lead, *dims):
    n = len(dims)
    return pl.BlockSpec(tuple(dims) + (HD,), lambda h: (0,) * n + (h,))


Q_SPEC = pl.BlockSpec((U, T, HD), lambda h: (0, 0, h))
KV_SPEC = pl.BlockSpec((U, 2, T, HD), lambda h: (0, 0, 0, h))
OT_SPEC = pl.BlockSpec((HD, 2 * ROWS), lambda h: (h, 0))
ST_SPEC = pl.BlockSpec((1, 8, 2 * ROWS), lambda h: (h, 0, 0))
ROW_SPEC = pl.BlockSpec((ROWS, HD), lambda h: (0, h))
PARAMS = pltpu.CompilerParams(vmem_limit_bytes=VMEM, dimension_semantics=("arbitrary",))


def struct(shape, dtype):
    return jax.ShapeDtypeStruct(shape, dtype)


def cost(flops, nbytes):
    return pl.CostEstimate(flops=flops, bytes_accessed=nbytes, transcendentals=0)


def forward(qa, qb, kv0, kv1, kv2, k3, v3):
    return pl.pallas_call(
        forward_kernel,
        grid=(HEADS,),
        in_specs=[Q_SPEC, Q_SPEC, KV_SPEC, KV_SPEC, KV_SPEC, Q_SPEC, Q_SPEC],
        out_specs=[OT_SPEC, ST_SPEC],
        out_shape=[struct((W, 2 * ROWS), F32), struct((HEADS, 8, 2 * ROWS), F32)],
        compiler_params=PARAMS,
        cost_estimate=cost(2 * 2 * 1024 * 2048 * W, 6 << 20),
        name="attn_forward",
    )(qa, qb, kv0, kv1, kv2, k3, v3)


def dot_kernel(ot_ref, st_ref, da, db, out_ref):
    out_ref[0, 0:2] = st_ref[0, 0:2]
    for part, d in enumerate((da, db)):
        at = slice(part * ROWS, (part + 1) * ROWS)
        grad_t = d[...].astype(F32).T
        out_ref[0, 2:3, at] = jnp.sum(grad_t * ot_ref[:, at], axis=0, keepdims=True)


def row_dots(ot, st, da, db):
    return pl.pallas_call(
        dot_kernel,
        grid=(HEADS,),
        in_specs=[OT_SPEC, ST_SPEC, ROW_SPEC, ROW_SPEC],
        out_specs=ST_SPEC,
        out_shape=struct((HEADS, 8, 2 * ROWS), F32),
        compiler_params=PARAMS,
        cost_estimate=cost(1 << 20, 3 << 20),
        name="row_dots",
    )(ot, st, da, db)


def merge_kernel(ot_ref, st_ref, pst_ref, keep_ref, send_ref, fin_ref):
    mine = st_ref[0]
    other = pst_ref[0]
    other = jnp.concatenate([other[:, ROWS:], other[:, :ROWS]], axis=1)
    top = jnp.maximum(mine[0:1], other[0:1])
    a = jnp.exp2(mine[0:1] - top)
    b = jnp.exp2(other[0:1] - top)
    total = a * mine[1:2] + b * other[1:2]
    fin_ref[0, 0:1] = top + jnp.log2(total)
    fin_ref[0, 1:2] = (a * mine[2:3] + b * other[2:3]) / total
    out_t = ot_ref[...] * (a / total)
    keep_ref[...] = out_t[:, :ROWS].T
    send_ref[...] = out_t[:, ROWS:].T.astype(BF)


def merge(ot, st, pst):
    return pl.pallas_call(
        merge_kernel,
        grid=(HEADS,),
        in_specs=[OT_SPEC, ST_SPEC, ST_SPEC],
        out_specs=[ROW_SPEC, ROW_SPEC, ST_SPEC],
        out_shape=[struct((ROWS, W), F32), struct((ROWS, W), BF), struct((HEADS, 8, 2 * ROWS), F32)],
        compiler_params=PARAMS,
        cost_estimate=cost(1 << 20, 3 << 20),
        name="merge_halves",
    )(ot, st, pst)


CHUNK = 256


def backward_block(keys, values, queries, grads, log_total, row_dot):
    scores = nt(keys, queries)
    probs = jnp.exp2(scores * SCALE2 - log_total)
    grad_probs = nt(values, grads)
    grad_scores = (probs * (grad_probs - row_dot)).astype(BF)
    grad_values = nn(probs.astype(BF), grads)
    grad_keys = nn(grad_scores, queries) * SCALE
    grad_queries_t = nn(keys.T, grad_scores)
    return grad_keys, grad_values, grad_queries_t


def backward_common(qa, qb, da, db, fin):
    queries = jnp.concatenate([flat(qa), flat(qb)], axis=0)
    grads = jnp.concatenate([da[...], db[...]], axis=0)
    return queries, grads, fin[0, 0:1], fin[0, 1:2]


def chunks_of(x):
    return [x[i * CHUNK : (i + 1) * CHUNK] for i in range(ROWS // CHUNK)]


def run_block(keys, values, common):
    dks, dvs, dqt = [], [], None
    for k, v in zip(chunks_of(keys), chunks_of(values)):
        dk, dv, q = backward_block(k, v, *common)
        dks.append(dk)
        dvs.append(dv)
        dqt = q if dqt is None else dqt + q
    return jnp.concatenate(dks, axis=0), jnp.concatenate(dvs, axis=0), dqt


def far_kernel(qa, qb, da, db, fin, k3, v3, dk_ref, dv_ref, dqt_ref):
    common = backward_common(qa, qb, da, db, fin)
    dk, dv, dqt = run_block(flat(k3), flat(v3), common)
    dk_ref[...] = dk.astype(BF).reshape(U, T, HD)
    dv_ref[...] = dv.astype(BF).reshape(U, T, HD)
    dqt_ref[...] = dqt


def near_kernel(qa, qb, da, db, fin, kv1, kv2, dqt_in, o1_ref, o2_ref, dqt_ref):
    common = backward_common(qa, qb, da, db, fin)
    total = dqt_in[...]
    for kv, o in ((kv1, o1_ref), (kv2, o2_ref)):
        dk, dv, dqt = run_block(kv[:, 0].reshape(ROWS, HD), kv[:, 1].reshape(ROWS, HD), common)
        o[:, 0] = dk.astype(o.dtype).reshape(U, T, HD)
        o[:, 1] = dv.astype(o.dtype).reshape(U, T, HD)
        total = total + dqt
    dqt_ref[...] = total


def own_kernel(qa, qb, da, db, fin, kv0, dqt_in, o0_ref, qkeep_ref, qsend_ref):
    common = backward_common(qa, qb, da, db, fin)
    dk, dv, dqt = run_block(kv0[:, 0].reshape(ROWS, HD), kv0[:, 1].reshape(ROWS, HD), common)
    o0_ref[:, 0] = dk.reshape(U, T, HD)
    o0_ref[:, 1] = dv.reshape(U, T, HD)
    total = (dqt_in[...] + dqt) * SCALE
    qkeep_ref[...] = total[:, :ROWS].T.reshape(U, T, HD)
    qsend_ref[...] = total[:, ROWS:].T.astype(BF).reshape(U, T, HD)


COMMON_SPECS = [Q_SPEC, Q_SPEC, ROW_SPEC, ROW_SPEC, ST_SPEC]


def backward_far(common, k3, v3):
    return pl.pallas_call(
        far_kernel,
        grid=(HEADS,),
        in_specs=COMMON_SPECS + [Q_SPEC, Q_SPEC],
        out_specs=[Q_SPEC, Q_SPEC, OT_SPEC],
        out_shape=[struct((U, T, W), BF), struct((U, T, W), BF), struct((W, 2 * ROWS), F32)],
        compiler_params=PARAMS,
        cost_estimate=cost(5 * 2 * 1024 * 512 * W, 6 << 20),
        name="backward_far",
    )(*common, k3, v3)


def backward_near(common, kv1, kv2, dqt):
    return pl.pallas_call(
        near_kernel,
        grid=(HEADS,),
        in_specs=COMMON_SPECS + [KV_SPEC, KV_SPEC, OT_SPEC],
        out_specs=[KV_SPEC, KV_SPEC, OT_SPEC],
        out_shape=[struct((U, 2, T, W), F32), struct((U, 2, T, W), F32), struct((W, 2 * ROWS), F32)],
        compiler_params=PARAMS,
        cost_estimate=cost(5 * 2 * 1024 * 1024 * W, 9 << 20),
        name="backward_near",
    )(*common, kv1, kv2, dqt)


def backward_own(common, kv0, dqt):
    return pl.pallas_call(
        own_kernel,
        grid=(HEADS,),
        in_specs=COMMON_SPECS + [KV_SPEC, OT_SPEC],
        out_specs=[KV_SPEC, Q_SPEC, Q_SPEC],
        out_shape=[struct((U, 2, T, W), F32), struct((U, T, W), F32), struct((U, T, W), BF)],
        compiler_params=PARAMS,
        cost_estimate=cost(5 * 2 * 1024 * 512 * W, 8 << 20),
        name="backward_own",
    )(*common, kv0, dqt)


def move(x, axis, to, n):
    return lax.ppermute(x, axis, [(i, to(i)) for i in range(n)])


def y_shift(x, d):
    return move(x, "blk", lambda i: i // 4 * 4 + (i + d) % 4, 8)


def z_swap(x):
    return move(x, "blk", lambda i: (i + 4) % 8, 8)


def to_heads(*rows):
    parts = [r.reshape(T, U, 1, W) for r in rows]
    stacked = jnp.concatenate(parts, axis=2) if len(parts) > 1 else parts[0]
    return lax.all_to_all(jnp.transpose(stacked, (1, 2, 0, 3)), "uly", split_axis=0, concat_axis=0, tiled=True)


def to_tokens(x):
    got = lax.all_to_all(x, "uly", split_axis=0, concat_axis=0, tiled=True)
    return [jnp.transpose(got[:, i], (1, 0, 2)).reshape(T, U * W) for i in range(x.shape[1])]


def per_device(query_rows, key_rows, value_rows, out_grad, out_weight):
    grad_block = lax.all_gather(out_grad, "uly", axis=0, tiled=True)
    weight = lax.all_gather(out_weight, ("dp", "blk"), axis=0, tiled=True)
    kv0 = to_heads(key_rows, value_rows)
    kv_prev = y_shift(kv0, 1)
    kv_next = y_shift(kv0, -1)
    qa = to_heads(query_rows)[:, 0]
    qb = z_swap(qa)
    k_far = y_shift(kv_prev[:, 0], 1)
    v_far = y_shift(kv_next[:, 1], -1)
    ot, st = forward(qa, qb, kv0, kv_prev, kv_next, k_far, v_far)
    da = nn(grad_block, weight).astype(BF)
    db = z_swap(da)
    st = row_dots(ot, st, da, db)
    pst = z_swap(st)
    o_keep, o_send, fin = merge(ot, st, pst)
    attn_out = (o_keep + z_swap(o_send).astype(F32)).astype(BF)

    common = (qa, qb, da, db, fin)
    dk_far, dv_far, dqt = backward_far(common, k_far, v_far)
    k_got = y_shift(dk_far, 1)
    v_got = y_shift(dv_far, -1)
    g_prev, g_next, dqt = backward_near(common, kv_prev, kv_next, dqt)
    add_k = jnp.stack([k_got, jnp.zeros_like(k_got)], axis=1).astype(F32)
    add_v = jnp.stack([jnp.zeros_like(v_got), v_got], axis=1).astype(F32)
    from_prev = y_shift((g_next + add_k).astype(BF), 1)
    from_next = y_shift((g_prev + add_v).astype(BF), -1)
    g_own, q_keep, q_send = backward_own(common, kv0, dqt)
    dq = (q_keep + z_swap(q_send).astype(F32)).astype(BF)
    (grad_query,) = to_tokens(dq[:, None])
    dkv = (g_own + from_prev.astype(F32) + from_next.astype(F32)).astype(BF)
    grad_key, grad_value = to_tokens(dkv)

    partial = lax.dot_general(grad_block, attn_out, (((0,), (0,)), ((), ())), preferred_element_type=F32)
    pieces = lax.all_to_all(partial.astype(BF), ("dp", "blk"), split_axis=0, concat_axis=0, tiled=True)
    grad_weight = jnp.sum(pieces.reshape(16, 320, W).astype(F32), axis=0)
    return (grad_query, grad_key, grad_value, grad_weight)


def solution(mesh):
    rows = P(("dp", "blk", "uly"), None)
    weight = P(("dp", "blk"), "uly")
    return jax.shard_map(
        per_device,
        mesh=mesh,
        in_specs=(rows, rows, rows, rows, weight),
        out_specs=(rows, rows, rows, weight),
        check_vma=False,
    )
```

```python
import functools

import jax
import jax.numpy as jnp
from jax import lax
from jax.experimental import pallas as pl
from jax.experimental.pallas import tpu as pltpu
from jax.sharding import PartitionSpec as P

HD = 128
HEADS = 3
U = 8
T = 64
W = HEADS * HD
ROWS = U * T
SCALE = HD**-0.5
SCALE2 = SCALE * 1.4426950408889634
BF = jnp.bfloat16
F32 = jnp.float32
VMEM = 60 * 1024 * 1024


def nt(a, b):
    return lax.dot_general(a, b, (((1,), (1,)), ((), ())), preferred_element_type=F32)


def nn(a, b):
    return jnp.dot(a, b, preferred_element_type=F32)


def flat(ref):
    return ref[...].reshape(ROWS, HD)


def joined(low, high, i):
    return jnp.concatenate([low[:, i].reshape(ROWS // 2, HD), high[:, i].reshape(ROWS // 2, HD)], axis=0)


def forward_kernel(qa, qb, kv0, kv1, kv2, kv3a, kv3b, ot_ref, st_ref):
    queries = jnp.concatenate([flat(qa), flat(qb)], axis=0)
    keys = [r[:, 0].reshape(ROWS, HD) for r in (kv0, kv1, kv2)] + [joined(kv3a, kv3b, 0)]
    values = [r[:, 1].reshape(ROWS, HD) for r in (kv0, kv1, kv2)] + [joined(kv3a, kv3b, 1)]
    later = nt(keys[0], queries)
    top = total = acc = None
    for j in range(4):
        scores = later
        if j < 3:
            later = nt(keys[j + 1], queries)
        peak = jnp.max(scores, axis=0, keepdims=True) * SCALE2
        if j > 0:
            peak = jnp.maximum(peak, top)
        weights = jnp.exp2(scores * SCALE2 - peak)
        sums = jnp.sum(weights, axis=0, keepdims=True)
        out = nn(values[j].T, weights.astype(BF))
        if j > 0:
            fade = jnp.exp2(top - peak)
            sums = sums + total * fade
            out = out + acc * fade
        top, total, acc = peak, sums, out
    st_ref[0, 0:1] = top
    st_ref[0, 1:2] = total
    ot_ref[...] = acc


Q_SPEC = pl.BlockSpec((U, T, HD), lambda h: (0, 0, h))
KV_SPEC = pl.BlockSpec((U, 2, T, HD), lambda h: (0, 0, 0, h))
HALF_SPEC = pl.BlockSpec((U // 2, 2, T, HD), lambda h: (0, 0, 0, h))
OT_SPEC = pl.BlockSpec((HD, 2 * ROWS), lambda h: (h, 0))
ST_SPEC = pl.BlockSpec((1, 8, 2 * ROWS), lambda h: (h, 0, 0))
ROW_SPEC = pl.BlockSpec((ROWS, HD), lambda h: (0, h))
SMALL_VMEM = 24 * 1024 * 1024
PARAMS = pltpu.CompilerParams(vmem_limit_bytes=VMEM, dimension_semantics=("arbitrary",))
SMALL = pltpu.CompilerParams(vmem_limit_bytes=SMALL_VMEM, dimension_semantics=("arbitrary",))


def struct(shape, dtype):
    return jax.ShapeDtypeStruct(shape, dtype)


def cost(flops, nbytes):
    return pl.CostEstimate(flops=flops, bytes_accessed=nbytes, transcendentals=0)


def forward(qa, qb, kv0, kv1, kv2, kv3a, kv3b):
    return pl.pallas_call(
        forward_kernel,
        grid=(HEADS,),
        in_specs=[Q_SPEC, Q_SPEC, KV_SPEC, KV_SPEC, KV_SPEC, HALF_SPEC, HALF_SPEC],
        out_specs=[OT_SPEC, ST_SPEC],
        out_shape=[struct((W, 2 * ROWS), F32), struct((HEADS, 8, 2 * ROWS), F32)],
        compiler_params=PARAMS,
        cost_estimate=cost(2 * 2 * 1024 * 2048 * W, 6 << 20),
        name="attn_forward",
    )(qa, qb, kv0, kv1, kv2, kv3a, kv3b)


def merge_kernel(ot_ref, st_ref, pst_ref, keep_ref, send_ref, fin_ref):
    mine = st_ref[0]
    other = halves_swapped(pst_ref[0])
    top = jnp.maximum(mine[0:1], other[0:1])
    a = jnp.exp2(mine[0:1] - top)
    b = jnp.exp2(other[0:1] - top)
    total = a * mine[1:2] + b * other[1:2]
    factor = a / total
    fin_ref[0, 0:1] = top + jnp.log2(total)
    fin_ref[0, 1:2] = factor
    out_t = ot_ref[...] * factor
    keep_ref[...] = out_t[:, :ROWS].T
    send_ref[...] = out_t[:, ROWS:].T.astype(BF)


def halves_swapped(x):
    return jnp.concatenate([x[:, ROWS:], x[:, :ROWS]], axis=1)


def merge(ot, st, pst):
    return pl.pallas_call(
        merge_kernel,
        grid=(HEADS,),
        in_specs=[OT_SPEC, ST_SPEC, ST_SPEC],
        out_specs=[ROW_SPEC, ROW_SPEC, ST_SPEC],
        out_shape=[struct((ROWS, W), F32), struct((ROWS, W), BF), struct((HEADS, 8, 2 * ROWS), F32)],
        compiler_params=SMALL,
        cost_estimate=cost(1 << 20, 3 << 20),
        name="merge_halves",
    )(ot, st, pst)


def dot_kernel(ot_ref, fin_ref, da, db, out_ref):
    for part, d in enumerate((da, db)):
        at = slice(part * ROWS, (part + 1) * ROWS)
        grad_t = d[...].astype(F32).T
        sums = jnp.sum(grad_t * ot_ref[:, at], axis=0, keepdims=True)
        out_ref[0, 0:1, at] = sums * fin_ref[0, 1:2, at]


def row_dots(ot, fin, da, db):
    return pl.pallas_call(
        dot_kernel,
        grid=(HEADS,),
        in_specs=[OT_SPEC, ST_SPEC, ROW_SPEC, ROW_SPEC],
        out_specs=ST_SPEC,
        out_shape=struct((HEADS, 8, 2 * ROWS), F32),
        compiler_params=SMALL,
        cost_estimate=cost(1 << 20, 3 << 20),
        name="row_dots",
    )(ot, fin, da, db)


FEATURES = 5120
QUARTER = FEATURES // 4
SHARD = FEATURES // 16
ANY_SPEC = pl.BlockSpec(memory_space=pl.ANY)
SMEM_SPEC = pl.BlockSpec(memory_space=pltpu.SMEM)
VMEM_SPEC = pl.BlockSpec(memory_space=pltpu.VMEM)
PLAIN = pltpu.CompilerParams(vmem_limit_bytes=VMEM)
PIECES = 10


def token_rows(place, piece):
    offset = (0, 1, 3, 2, 2)[piece % 5]
    x = lax.rem(place[0] + offset, 4)
    core = place[1] if piece < 5 else 1 - place[1]
    first = (x * 2 + core) * T + (T // 2 if piece % 5 == 4 else 0)
    return pl.multiple_of(first, T // 2), (T if piece % 5 < 3 else T // 2)


def grad_copies(place, pieces, held, sems, columns):
    copies = []
    for i, piece in enumerate(pieces):
        first, rows = token_rows(place, i)
        copies.append(pltpu.make_async_copy(piece.at[:, columns], held.at[pl.ds(first, rows)], sems.at[i]))
    return copies


def stack_kernel(*refs):
    for i, piece in enumerate(refs[:4]):
        refs[4][i * SHARD : (i + 1) * SHARD] = piece[...]


def stacked_rows(*pieces):
    return pl.pallas_call(
        stack_kernel,
        in_specs=[VMEM_SPEC] * 4,
        out_specs=VMEM_SPEC,
        out_shape=struct((QUARTER, W), BF),
        compiler_params=pltpu.CompilerParams(vmem_limit_bytes=SMALL_VMEM),
        cost_estimate=cost(0, 2 << 20),
        name="stack_rows",
    )(*pieces)


def project_kernel(place, *refs):
    pieces, (w0, w1, w2a, w2b, w3), (out_ref, held, weight, sems) = refs[:PIECES], refs[PIECES : PIECES + 5], refs[PIECES + 5 :]
    groups = []
    for oz in range(4):
        quarter = lax.rem(place[2] + oz, 4)
        columns = pl.ds(pl.multiple_of(quarter * QUARTER, 128), QUARTER)
        copies = grad_copies(place, pieces, held.at[oz], sems.at[oz], columns)
        for oy in range(4):
            source, row = ((w0, oy), (w1, oy), (w2a, oy) if oy < 2 else (w2b, oy - 2), (w3, oy))[oz]
            at = pl.multiple_of(lax.rem(place[3] + oy, 4) * SHARD, SHARD)
            target = weight.at[oz, pl.ds(at, SHARD)]
            copies.append(pltpu.make_async_copy(source.at[pl.ds(row * SHARD, SHARD)], target, sems.at[oz, PIECES + oy]))
        for c in copies:
            c.start()
        groups.append(copies)
    total = None
    for oz in range(4):
        for c in groups[oz]:
            c.wait()
        part = nn(held[oz], weight[oz])
        total = part if total is None else total + part
    out_ref[...] = total.astype(BF)


def project(place, pieces, weights):
    return pl.pallas_call(
        project_kernel,
        in_specs=[SMEM_SPEC] + [ANY_SPEC] * (PIECES + 5),
        out_specs=VMEM_SPEC,
        out_shape=struct((ROWS, W), BF),
        scratch_shapes=[
            pltpu.VMEM((4, ROWS, QUARTER), BF),
            pltpu.VMEM((4, QUARTER, W), BF),
            pltpu.SemaphoreType.DMA((4, PIECES + 4)),
        ],
        compiler_params=PLAIN,
        cost_estimate=cost(2 * ROWS * FEATURES * W, 10 << 20),
        name="project",
    )(place, *pieces, *weights)


def tn(a, b):
    return lax.dot_general(a, b, (((0,), (0,)), ((), ())), preferred_element_type=F32)


def weight_part(place, oz, pieces, attn, held, sems):
    at = lax.rem(place[2] + oz, 4) * QUARTER
    copies = grad_copies(place, pieces, held, sems, pl.ds(pl.multiple_of(at, 128), QUARTER))
    for c in copies:
        c.start()
    for c in copies:
        c.wait()
    return tn(held[...], attn[...])


def weight_far_kernel(place, *refs):
    pieces, (attn, a_ref, b_ref, held, sems) = refs[:PIECES], refs[PIECES:]
    part = weight_part(place, 2, pieces, attn, held, sems).astype(BF)
    a_ref[...] = part[: QUARTER // 2]
    b_ref[...] = part[QUARTER // 2 :]


def weight_near_kernel(place, *refs):
    pieces, (attn, a_got, b_got, up_ref, down_ref, held, sems) = refs[:PIECES], refs[PIECES:]
    half = QUARTER // 2
    part = weight_part(place, 1, pieces, attn, held, sems)
    up_ref[:half] = (part[:half] + a_got[...].astype(F32)).astype(BF)
    up_ref[half:] = part[half:].astype(BF)
    part = weight_part(place, 3, pieces, attn, held, sems)
    down_ref[:half] = part[:half].astype(BF)
    down_ref[half:] = (part[half:] + b_got[...].astype(F32)).astype(BF)


def weight_own_kernel(place, *refs):
    pieces, (attn, below, above, o0, o1, o2, o3, held, sems, total) = refs[:PIECES], refs[PIECES:]
    part = weight_part(place, 0, pieces, attn, held, sems)
    total[...] = part + below[...].astype(F32) + above[...].astype(F32)
    for oy, o in enumerate((o0, o1, o2, o3)):
        at = pl.multiple_of(lax.rem(place[3] + oy, 4) * SHARD, SHARD)
        o[...] = total[pl.ds(at, SHARD)].astype(o.dtype)


def weight_call(kernel, name, parts, outs, extra, place, pieces, *more):
    return pl.pallas_call(
        kernel,
        in_specs=[SMEM_SPEC] + [ANY_SPEC] * PIECES + [VMEM_SPEC] * len(more),
        out_specs=[VMEM_SPEC] * len(outs),
        out_shape=outs,
        scratch_shapes=[pltpu.VMEM((ROWS, QUARTER), BF), pltpu.SemaphoreType.DMA((PIECES,))] + extra,
        compiler_params=PLAIN,
        cost_estimate=cost(parts * 2 * ROWS * QUARTER * W, parts * 3 << 20),
        name=name,
    )(place, *pieces, *more)


CHUNK = 256


def backward_block(keys, values, queries, grads, log_total, row_dot):
    scores = nt(keys, queries)
    probs = jnp.exp2(scores * SCALE2 - log_total)
    grad_probs = nt(values, grads)
    grad_scores = (probs * (grad_probs - row_dot)).astype(BF)
    grad_values = nn(probs.astype(BF), grads)
    grad_keys = nn(grad_scores, queries) * SCALE
    grad_queries_t = nn(keys.T, grad_scores)
    return grad_keys, grad_values, grad_queries_t


def backward_common(qa, qb, da, db, fin, dots, pdots):
    queries = jnp.concatenate([flat(qa), flat(qb)], axis=0)
    grads = jnp.concatenate([da[...], db[...]], axis=0)
    row_dot = dots[0, 0:1] + halves_swapped(pdots[0, 0:1])
    return queries, grads, fin[0, 0:1], row_dot


def chunks_of(x):
    return [x[i * CHUNK : (i + 1) * CHUNK] for i in range(ROWS // CHUNK)]


def run_block(keys, values, common):
    dks, dvs, dqt = [], [], None
    for k, v in zip(chunks_of(keys), chunks_of(values)):
        dk, dv, q = backward_block(k, v, *common)
        dks.append(dk)
        dvs.append(dv)
        dqt = q if dqt is None else dqt + q
    return jnp.concatenate(dks, axis=0), jnp.concatenate(dvs, axis=0), dqt


def store_halves(low, high, i, x):
    low[:, i] = x[: ROWS // 2].astype(low.dtype).reshape(U // 2, T, HD)
    high[:, i] = x[ROWS // 2 :].astype(high.dtype).reshape(U // 2, T, HD)


def far_kernel(qa, qb, da, db, fin, dots, pdots, kv3a, kv3b, low_ref, high_ref, dqt_ref):
    common = backward_common(qa, qb, da, db, fin, dots, pdots)
    dk, dv, dqt = run_block(joined(kv3a, kv3b, 0), joined(kv3a, kv3b, 1), common)
    store_halves(low_ref, high_ref, 0, dk)
    store_halves(low_ref, high_ref, 1, dv)
    dqt_ref[...] = dqt


def near_kernel(qa, qb, da, db, fin, dots, pdots, kv1, kv2, dqt_in, l1_ref, h1_ref, l2_ref, h2_ref, dqt_ref):
    common = backward_common(qa, qb, da, db, fin, dots, pdots)
    total = dqt_in[...]
    for kv, low, high in ((kv1, l1_ref, h1_ref), (kv2, l2_ref, h2_ref)):
        dk, dv, dqt = run_block(kv[:, 0].reshape(ROWS, HD), kv[:, 1].reshape(ROWS, HD), common)
        store_halves(low, high, 0, dk)
        store_halves(low, high, 1, dv)
        total = total + dqt
    dqt_ref[...] = total


def own_kernel(qa, qb, da, db, fin, dots, pdots, kv0, dqt_in, o0_ref, qkeep_ref, qsend_ref):
    common = backward_common(qa, qb, da, db, fin, dots, pdots)
    dk, dv, dqt = run_block(kv0[:, 0].reshape(ROWS, HD), kv0[:, 1].reshape(ROWS, HD), common)
    o0_ref[:, 0] = dk.reshape(U, T, HD)
    o0_ref[:, 1] = dv.reshape(U, T, HD)
    total = (dqt_in[...] + dqt) * SCALE
    qkeep_ref[...] = total[:, :ROWS].T.reshape(U, T, HD)
    qsend_ref[...] = total[:, ROWS:].T.astype(BF).reshape(U, T, HD)


COMMON_SPECS = [Q_SPEC, Q_SPEC, ROW_SPEC, ROW_SPEC, ST_SPEC, ST_SPEC, ST_SPEC]


def backward_far(common, kv3a, kv3b):
    return pl.pallas_call(
        far_kernel,
        grid=(HEADS,),
        in_specs=COMMON_SPECS + [HALF_SPEC, HALF_SPEC],
        out_specs=[HALF_SPEC, HALF_SPEC, OT_SPEC],
        out_shape=[struct((U // 2, 2, T, W), BF)] * 2 + [struct((W, 2 * ROWS), F32)],
        compiler_params=PARAMS,
        cost_estimate=cost(5 * 2 * 1024 * 512 * W, 6 << 20),
        name="backward_far",
    )(*common, kv3a, kv3b)


def backward_near(common, kv1, kv2, dqt):
    return pl.pallas_call(
        near_kernel,
        grid=(HEADS,),
        in_specs=COMMON_SPECS + [KV_SPEC, KV_SPEC, OT_SPEC],
        out_specs=[HALF_SPEC] * 4 + [OT_SPEC],
        out_shape=[struct((U // 2, 2, T, W), t) for t in (BF, F32, F32, BF)] + [struct((W, 2 * ROWS), F32)],
        compiler_params=PARAMS,
        cost_estimate=cost(5 * 2 * 1024 * 1024 * W, 9 << 20),
        name="backward_near",
    )(*common, kv1, kv2, dqt)


def backward_own(common, kv0, dqt):
    return pl.pallas_call(
        own_kernel,
        grid=(HEADS,),
        in_specs=COMMON_SPECS + [KV_SPEC, OT_SPEC],
        out_specs=[KV_SPEC, Q_SPEC, Q_SPEC],
        out_shape=[struct((U, 2, T, W), F32), struct((U, T, W), F32), struct((U, T, W), BF)],
        compiler_params=PARAMS,
        cost_estimate=cost(5 * 2 * 1024 * 512 * W, 8 << 20),
        name="backward_own",
    )(*common, kv0, dqt)


def move(x, axis, to, n):
    return lax.ppermute(x, axis, [(i, to(i)) for i in range(n)])


def y_shift(x, d):
    return move(x, "blk", lambda i: i // 4 * 4 + (i + d) % 4, 8)


def z_shift(x, d):
    return move(x, ("dp", "blk"), lambda i: (i // 4 + d) % 4 * 4 + i % 4, 16)


def x_shift(x, d):
    return move(x, "uly", lambda i: (i // 2 + d) % 4 * 2 + i % 2, 8)


def core_swap(x):
    return move(x, "uly", lambda i: i ^ 1, 8)


def z_swap(x):
    return move(x, "blk", lambda i: (i + 4) % 8, 8)


def by_head(*rows):
    stacked = jnp.concatenate([r.reshape(T, U, 1, W) for r in rows], axis=2)
    return jnp.transpose(stacked, (1, 2, 0, 3))


def exchange(x):
    return lax.all_to_all(x, "uly", split_axis=0, concat_axis=0, tiled=True)


def to_tokens(x):
    got = exchange(x)
    return [jnp.transpose(got[:, i], (1, 0, 2)).reshape(T, U * W) for i in range(x.shape[1])]


def after(x, *others):
    return lax.optimization_barrier((x, *others))[0]


def per_device(query_rows, key_rows, value_rows, out_grad, out_weight):
    uly, blk = lax.axis_index("uly"), lax.axis_index("blk")
    place = jnp.stack([uly // 2, uly % 2, lax.axis_index("dp") * 2 + blk // 4, blk % 4]).astype(jnp.int32)
    leaving = by_head(key_rows, value_rows, query_rows)
    shards = (out_weight, y_shift(out_weight, -1), y_shift(out_weight, 2), y_shift(out_weight, 1))
    grad_below, grad_above = x_shift(out_grad, 1), x_shift(out_grad, -1)
    heads = exchange(leaving)
    weight_own = stacked_rows(*after(shards, heads))
    kv0, qa = heads[:, :2], heads[:, 2]
    kv_prev, kv_next = y_shift(kv0, 1), y_shift(kv0, -1)
    qb = z_swap(qa)
    weight_below, weight_above = z_shift(weight_own, 1), z_shift(weight_own, -1)
    near_parts = (kv_prev[: U // 2], kv_next[U // 2 :])
    grad_parts = (grad_above[: T // 2], grad_below[T // 2 :])
    cut = QUARTER // 2
    weight_parts = (weight_above[:cut], weight_below[cut:])
    far_low, far_high = y_shift(near_parts[0], 1), y_shift(near_parts[1], -1)
    grad_far = [x_shift(grad_parts[0], -1), x_shift(grad_parts[1], 1)]
    weight_far = [z_shift(weight_parts[0], -1), z_shift(weight_parts[1], 1)]
    weights = (weight_own, weight_above, *weight_far, weight_below)
    mine = [out_grad, grad_above, grad_below] + grad_far
    pieces = mine + [core_swap(p) for p in mine]
    da = project(place, pieces, weights)
    db = z_swap(da)
    ot, st = forward(after(qa, da), qb, kv0, kv_prev, kv_next, far_low, far_high)
    pst = z_swap(st)
    o_keep, o_send, fin = merge(ot, st, pst)
    dots = row_dots(ot, fin, da, db)
    attn_out = (o_keep + z_swap(o_send).astype(F32)).astype(BF)
    common = (qa, qb, da, db, fin, dots, z_swap(dots))

    low, high, dqt = backward_far(common, far_low, far_high)
    low_got, high_got = y_shift(low, 1), y_shift(high, -1)
    half = struct((QUARTER // 2, W), BF)
    a, b = weight_call(weight_far_kernel, "weight_far", 1, [half, half], [], place, pieces, after(attn_out, dqt))
    a_got, b_got = z_shift(a, 1), z_shift(b, -1)
    prev_low, prev_high, next_low, next_high, dqt = backward_near(common, kv_prev, kv_next, after(dqt, a, b))
    high_below = y_shift(next_high, 1)
    low_above = y_shift(prev_low, -1)
    low_below = y_shift((next_low + low_got.astype(F32)).astype(BF), 1)
    high_above = y_shift((prev_high + high_got.astype(F32)).astype(BF), -1)
    g_own, q_keep, q_send = backward_own(common, kv0, dqt)
    whole = struct((QUARTER, W), BF)
    up, down = weight_call(
        weight_near_kernel, "weight_near", 2, [whole, whole], [], place, pieces, after(attn_out, q_send), a_got, b_got
    )
    below, above = z_shift(up, 1), z_shift(down, -1)
    dq = (q_keep + z_swap(q_send).astype(F32)).astype(BF)
    g_low = g_own[: U // 2] + low_below.astype(F32) + low_above.astype(F32)
    g_high = g_own[U // 2 :] + high_below.astype(F32) + high_above.astype(F32)
    dkv = jnp.concatenate([g_low.astype(BF), g_high.astype(BF)], axis=0)
    grads = jnp.concatenate([dkv, dq[:, None]], axis=1)
    grad_key, grad_value, grad_query = to_tokens(grads)
    o0, o1, o2, o3 = weight_call(
        weight_own_kernel,
        "weight_own",
        1,
        [struct((SHARD, W), F32)] + [struct((SHARD, W), BF)] * 3,
        [pltpu.VMEM((QUARTER, W), F32)],
        place,
        pieces,
        after(attn_out, grads),
        below,
        above,
    )
    grad_weight = o0 + y_shift(o1, 1).astype(F32) + y_shift(o2, 2).astype(F32) + y_shift(o3, -1).astype(F32)
    return (grad_query, grad_key, grad_value, grad_weight)


def solution(mesh):
    rows = P(("dp", "blk", "uly"), None)
    weight = P(("dp", "blk"), "uly")
    return jax.shard_map(
        per_device,
        mesh=mesh,
        in_specs=(rows, rows, rows, rows, weight),
        out_specs=(rows, rows, rows, weight),
        check_vma=False,
    )
```

```python
import functools

import jax
import jax.numpy as jnp
from jax import lax
from jax.experimental import pallas as pl
from jax.experimental.pallas import tpu as pltpu
from jax.sharding import PartitionSpec as P

HD = 128
HEADS = 3
U = 8
T = 64
W = HEADS * HD
ROWS = U * T
SCALE = HD**-0.5
SCALE2 = SCALE * 1.4426950408889634
BF = jnp.bfloat16
F32 = jnp.float32
VMEM = 60 * 1024 * 1024


def nt(a, b):
    return lax.dot_general(a, b, (((1,), (1,)), ((), ())), preferred_element_type=F32)


def nn(a, b):
    return jnp.dot(a, b, preferred_element_type=F32)


def flat(ref):
    return ref[...].reshape(ROWS, HD)


def joined(low, high, i):
    return jnp.concatenate([low[:, i].reshape(ROWS // 2, HD), high[:, i].reshape(ROWS // 2, HD)], axis=0)


def forward_blocks(queries, blocks, state):
    top, total, acc = state
    later = nt(blocks[0][0], queries)
    for j, (_, values) in enumerate(blocks):
        scores = later
        if j + 1 < len(blocks):
            later = nt(blocks[j + 1][0], queries)
        peak = jnp.max(scores, axis=0, keepdims=True) * SCALE2
        if top is not None:
            peak = jnp.maximum(peak, top)
        weights = jnp.exp2(scores * SCALE2 - peak)
        sums = jnp.sum(weights, axis=0, keepdims=True)
        out = nn(values.T, weights.astype(BF))
        if top is not None:
            fade = jnp.exp2(top - peak)
            sums = sums + total * fade
            out = out + acc * fade
        top, total, acc = peak, sums, out
    return top, total, acc


def forward_near_kernel(qa, qb, kv0, kv1, kv2, ot_ref, st_ref):
    queries = jnp.concatenate([flat(qa), flat(qb)], axis=0)
    blocks = [(r[:, 0].reshape(ROWS, HD), r[:, 1].reshape(ROWS, HD)) for r in (kv0, kv1, kv2)]
    st_ref[0, 0:1], st_ref[0, 1:2], ot_ref[...] = forward_blocks(queries, blocks, (None, None, None))


def forward_far_kernel(qa, qb, kv3a, kv3b, ot_in, st_in, ot_ref, st_ref):
    queries = jnp.concatenate([flat(qa), flat(qb)], axis=0)
    blocks = [(joined(kv3a, kv3b, 0), joined(kv3a, kv3b, 1))]
    state = (st_in[0, 0:1], st_in[0, 1:2], ot_in[...])
    st_ref[0, 0:1], st_ref[0, 1:2], ot_ref[...] = forward_blocks(queries, blocks, state)


Q_SPEC = pl.BlockSpec((U, T, HD), lambda h: (0, 0, h))
KV_SPEC = pl.BlockSpec((U, 2, T, HD), lambda h: (0, 0, 0, h))
HALF_SPEC = pl.BlockSpec((U // 2, 2, T, HD), lambda h: (0, 0, 0, h))
OT_SPEC = pl.BlockSpec((HD, 2 * ROWS), lambda h: (h, 0))
ST_SPEC = pl.BlockSpec((1, 8, 2 * ROWS), lambda h: (h, 0, 0))
ROW_SPEC = pl.BlockSpec((ROWS, HD), lambda h: (0, h))
SMALL_VMEM = 24 * 1024 * 1024
PARAMS = pltpu.CompilerParams(vmem_limit_bytes=VMEM, dimension_semantics=("arbitrary",))
SMALL = pltpu.CompilerParams(vmem_limit_bytes=SMALL_VMEM, dimension_semantics=("arbitrary",))


def struct(shape, dtype):
    return jax.ShapeDtypeStruct(shape, dtype)


def cost(flops, nbytes):
    return pl.CostEstimate(flops=flops, bytes_accessed=nbytes, transcendentals=0)


def forward_call(kernel, name, blocks, in_specs, operands):
    return pl.pallas_call(
        kernel,
        grid=(HEADS,),
        in_specs=in_specs,
        out_specs=[OT_SPEC, ST_SPEC],
        out_shape=[struct((W, 2 * ROWS), F32), struct((HEADS, 8, 2 * ROWS), F32)],
        compiler_params=PARAMS,
        cost_estimate=cost(blocks * 4 * 1024 * ROWS * W, (blocks + 2) << 20),
        name=name,
    )(*operands)


def forward_near(*operands):
    return forward_call(forward_near_kernel, "forward_near", 3, [Q_SPEC] * 2 + [KV_SPEC] * 3, operands)


def forward_far(*operands):
    specs = [Q_SPEC] * 2 + [HALF_SPEC] * 2 + [OT_SPEC, ST_SPEC]
    return forward_call(forward_far_kernel, "forward_far", 1, specs, operands)


def dot_kernel(ot_ref, st_ref, da, db, out_ref):
    out_ref[0, 0:2] = st_ref[0, 0:2]
    for part, d in enumerate((da, db)):
        at = slice(part * ROWS, (part + 1) * ROWS)
        grad_t = d[...].astype(F32).T
        out_ref[0, 2:3, at] = jnp.sum(grad_t * ot_ref[:, at], axis=0, keepdims=True)


def row_dots(ot, st, da, db):
    return pl.pallas_call(
        dot_kernel,
        grid=(HEADS,),
        in_specs=[OT_SPEC, ST_SPEC, ROW_SPEC, ROW_SPEC],
        out_specs=ST_SPEC,
        out_shape=struct((HEADS, 8, 2 * ROWS), F32),
        compiler_params=SMALL,
        cost_estimate=cost(1 << 20, 3 << 20),
        name="row_dots",
    )(ot, st, da, db)


def merge_kernel(ot_ref, st_ref, pst_ref, keep_ref, send_ref, fin_ref):
    mine = st_ref[0]
    other = pst_ref[0]
    other = jnp.concatenate([other[:, ROWS:], other[:, :ROWS]], axis=1)
    top = jnp.maximum(mine[0:1], other[0:1])
    a = jnp.exp2(mine[0:1] - top)
    b = jnp.exp2(other[0:1] - top)
    total = a * mine[1:2] + b * other[1:2]
    fin_ref[0, 0:1] = top + jnp.log2(total)
    fin_ref[0, 1:2] = (a * mine[2:3] + b * other[2:3]) / total
    out_t = ot_ref[...] * (a / total)
    keep_ref[...] = out_t[:, :ROWS].T
    send_ref[...] = out_t[:, ROWS:].T.astype(BF)


def merge(ot, st, pst):
    return pl.pallas_call(
        merge_kernel,
        grid=(HEADS,),
        in_specs=[OT_SPEC, ST_SPEC, ST_SPEC],
        out_specs=[ROW_SPEC, ROW_SPEC, ST_SPEC],
        out_shape=[struct((ROWS, W), F32), struct((ROWS, W), BF), struct((HEADS, 8, 2 * ROWS), F32)],
        compiler_params=SMALL,
        cost_estimate=cost(1 << 20, 3 << 20),
        name="merge_halves",
    )(ot, st, pst)


FEATURES = 5120
QUARTER = FEATURES // 4
SHARD = FEATURES // 16
ANY_SPEC = pl.BlockSpec(memory_space=pl.ANY)
SMEM_SPEC = pl.BlockSpec(memory_space=pltpu.SMEM)
VMEM_SPEC = pl.BlockSpec(memory_space=pltpu.VMEM)
PLAIN = pltpu.CompilerParams(vmem_limit_bytes=VMEM)


def stack_kernel(*refs):
    for i, piece in enumerate(refs[:4]):
        refs[4][i * SHARD : (i + 1) * SHARD] = piece[...]


def stacked_rows(*pieces):
    return pl.pallas_call(
        stack_kernel,
        in_specs=[VMEM_SPEC] * 4,
        out_specs=VMEM_SPEC,
        out_shape=struct((QUARTER, W), BF),
        compiler_params=pltpu.CompilerParams(vmem_limit_bytes=SMALL_VMEM),
        cost_estimate=cost(0, 2 << 20),
        name="stack_rows",
    )(*pieces)


def project_kernel(place, grad, w0, w1, w2a, w2b, w3, out_ref, held, weight, sems):
    groups = []
    for oz in range(4):
        quarter = lax.rem(place[2] + oz, 4)
        columns = pl.ds(pl.multiple_of(quarter * QUARTER, 128), QUARTER)
        copies = [pltpu.make_async_copy(grad.at[:, columns], held.at[oz], sems.at[oz, 4])]
        for oy in range(4):
            source, row = ((w0, oy), (w1, oy), (w2a, oy) if oy < 2 else (w2b, oy - 2), (w3, oy))[oz]
            at = pl.multiple_of(lax.rem(place[3] + oy, 4) * SHARD, SHARD)
            target = weight.at[oz, pl.ds(at, SHARD)]
            copies.append(pltpu.make_async_copy(source.at[pl.ds(row * SHARD, SHARD)], target, sems.at[oz, oy]))
        for c in copies:
            c.start()
        groups.append(copies)
    total = None
    for oz in range(4):
        for c in groups[oz]:
            c.wait()
        part = nn(held[oz], weight[oz])
        total = part if total is None else total + part
    out_ref[...] = total.astype(BF)


def project(place, grad, weights):
    return pl.pallas_call(
        project_kernel,
        in_specs=[SMEM_SPEC] + [ANY_SPEC] * 6,
        out_specs=VMEM_SPEC,
        out_shape=struct((ROWS, W), BF),
        scratch_shapes=[
            pltpu.VMEM((4, ROWS, QUARTER), BF),
            pltpu.VMEM((4, QUARTER, W), BF),
            pltpu.SemaphoreType.DMA((4, 5)),
        ],
        compiler_params=PLAIN,
        cost_estimate=cost(2 * ROWS * FEATURES * W, 10 << 20),
        name="project",
    )(place, grad, *weights)


def tn(a, b):
    return lax.dot_general(a, b, (((0,), (0,)), ((), ())), preferred_element_type=F32)


def weight_part(place, oz, grad, attn, held, sem):
    at = lax.rem(place[2] + oz, 4) * QUARTER
    copy = pltpu.make_async_copy(grad.at[:, pl.ds(pl.multiple_of(at, 128), QUARTER)], held, sem)
    copy.start()
    copy.wait()
    return tn(held[...], attn[...])


def weight_far_kernel(place, grad, attn, a_ref, b_ref, held, sem):
    part = weight_part(place, 2, grad, attn, held, sem).astype(BF)
    a_ref[...] = part[: QUARTER // 2]
    b_ref[...] = part[QUARTER // 2 :]


def weight_near_kernel(place, grad, attn, a_got, b_got, up_ref, down_ref, held, sem):
    half = QUARTER // 2
    part = weight_part(place, 1, grad, attn, held, sem)
    up_ref[:half] = (part[:half] + a_got[...].astype(F32)).astype(BF)
    up_ref[half:] = part[half:].astype(BF)
    part = weight_part(place, 3, grad, attn, held, sem)
    down_ref[:half] = part[:half].astype(BF)
    down_ref[half:] = (part[half:] + b_got[...].astype(F32)).astype(BF)


def weight_own_kernel(place, grad, attn, below, above, o0, o1, o2, o3, held, sem, total):
    part = weight_part(place, 0, grad, attn, held, sem)
    total[...] = part + below[...].astype(F32) + above[...].astype(F32)
    for oy, o in enumerate((o0, o1, o2, o3)):
        at = pl.multiple_of(lax.rem(place[3] + oy, 4) * SHARD, SHARD)
        o[...] = total[pl.ds(at, SHARD)].astype(o.dtype)


def weight_call(kernel, name, parts, outs, extra, place, grad, *more):
    return pl.pallas_call(
        kernel,
        in_specs=[SMEM_SPEC, ANY_SPEC] + [VMEM_SPEC] * len(more),
        out_specs=[VMEM_SPEC] * len(outs),
        out_shape=outs,
        scratch_shapes=[pltpu.VMEM((ROWS, QUARTER), BF), pltpu.SemaphoreType.DMA] + extra,
        compiler_params=PLAIN,
        cost_estimate=cost(parts * 2 * ROWS * QUARTER * W, parts * 3 << 20),
        name=name,
    )(place, grad, *more)


CHUNK = 256


def backward_block(keys, values, queries, grads, log_total, row_dot):
    scores = nt(keys, queries)
    probs = jnp.exp2(scores * SCALE2 - log_total)
    grad_probs = nt(values, grads)
    grad_scores = (probs * (grad_probs - row_dot)).astype(BF)
    grad_values = nn(probs.astype(BF), grads)
    grad_keys = nn(grad_scores, queries) * SCALE
    grad_queries_t = nn(keys.T, grad_scores)
    return grad_keys, grad_values, grad_queries_t


def backward_common(qa, qb, da, db, fin):
    queries = jnp.concatenate([flat(qa), flat(qb)], axis=0)
    grads = jnp.concatenate([da[...], db[...]], axis=0)
    return queries, grads, fin[0, 0:1], fin[0, 1:2]


def chunks_of(x):
    return [x[i * CHUNK : (i + 1) * CHUNK] for i in range(ROWS // CHUNK)]


def run_block(keys, values, common):
    dks, dvs, dqt = [], [], None
    for k, v in zip(chunks_of(keys), chunks_of(values)):
        dk, dv, q = backward_block(k, v, *common)
        dks.append(dk)
        dvs.append(dv)
        dqt = q if dqt is None else dqt + q
    return jnp.concatenate(dks, axis=0), jnp.concatenate(dvs, axis=0), dqt


def store_halves(low, high, i, x):
    low[:, i] = x[: ROWS // 2].astype(low.dtype).reshape(U // 2, T, HD)
    high[:, i] = x[ROWS // 2 :].astype(high.dtype).reshape(U // 2, T, HD)


def far_kernel(qa, qb, da, db, fin, kv3a, kv3b, low_ref, high_ref, dqt_ref):
    common = backward_common(qa, qb, da, db, fin)
    dk, dv, dqt = run_block(joined(kv3a, kv3b, 0), joined(kv3a, kv3b, 1), common)
    store_halves(low_ref, high_ref, 0, dk)
    store_halves(low_ref, high_ref, 1, dv)
    dqt_ref[...] = dqt


def near_kernel(qa, qb, da, db, fin, kv1, kv2, dqt_in, o1_ref, o2_ref, dqt_ref):
    common = backward_common(qa, qb, da, db, fin)
    total = dqt_in[...]
    for kv, o in ((kv1, o1_ref), (kv2, o2_ref)):
        dk, dv, dqt = run_block(kv[:, 0].reshape(ROWS, HD), kv[:, 1].reshape(ROWS, HD), common)
        o[:, 0] = dk.reshape(U, T, HD)
        o[:, 1] = dv.reshape(U, T, HD)
        total = total + dqt
    dqt_ref[...] = total


def own_kernel(qa, qb, da, db, fin, kv0, dqt_in, o0_ref, qkeep_ref, qsend_ref):
    common = backward_common(qa, qb, da, db, fin)
    dk, dv, dqt = run_block(kv0[:, 0].reshape(ROWS, HD), kv0[:, 1].reshape(ROWS, HD), common)
    o0_ref[:, 0] = dk.reshape(U, T, HD)
    o0_ref[:, 1] = dv.reshape(U, T, HD)
    total = (dqt_in[...] + dqt) * SCALE
    qkeep_ref[...] = total[:, :ROWS].T.reshape(U, T, HD)
    qsend_ref[...] = total[:, ROWS:].T.astype(BF).reshape(U, T, HD)


COMMON_SPECS = [Q_SPEC, Q_SPEC, ROW_SPEC, ROW_SPEC, ST_SPEC]


def backward_far(common, kv3a, kv3b):
    return pl.pallas_call(
        far_kernel,
        grid=(HEADS,),
        in_specs=COMMON_SPECS + [HALF_SPEC, HALF_SPEC],
        out_specs=[HALF_SPEC, HALF_SPEC, OT_SPEC],
        out_shape=[struct((U // 2, 2, T, W), BF)] * 2 + [struct((W, 2 * ROWS), F32)],
        compiler_params=PARAMS,
        cost_estimate=cost(5 * 2 * 1024 * 512 * W, 6 << 20),
        name="backward_far",
    )(*common, kv3a, kv3b)


def backward_near(common, kv1, kv2, dqt):
    return pl.pallas_call(
        near_kernel,
        grid=(HEADS,),
        in_specs=COMMON_SPECS + [KV_SPEC, KV_SPEC, OT_SPEC],
        out_specs=[KV_SPEC, KV_SPEC, OT_SPEC],
        out_shape=[struct((U, 2, T, W), F32)] * 2 + [struct((W, 2 * ROWS), F32)],
        compiler_params=PARAMS,
        cost_estimate=cost(5 * 2 * 1024 * 1024 * W, 9 << 20),
        name="backward_near",
    )(*common, kv1, kv2, dqt)


def backward_own(common, kv0, dqt):
    return pl.pallas_call(
        own_kernel,
        grid=(HEADS,),
        in_specs=COMMON_SPECS + [KV_SPEC, OT_SPEC],
        out_specs=[KV_SPEC, Q_SPEC, Q_SPEC],
        out_shape=[struct((U, 2, T, W), F32), struct((U, T, W), F32), struct((U, T, W), BF)],
        compiler_params=PARAMS,
        cost_estimate=cost(5 * 2 * 1024 * 512 * W, 8 << 20),
        name="backward_own",
    )(*common, kv0, dqt)


def move(x, axis, to, n):
    return lax.ppermute(x, axis, [(i, to(i)) for i in range(n)])


def y_shift(x, d):
    return move(x, "blk", lambda i: i // 4 * 4 + (i + d) % 4, 8)


def z_shift(x, d):
    return move(x, ("dp", "blk"), lambda i: (i // 4 + d) % 4 * 4 + i % 4, 16)


def z_swap(x):
    return move(x, "blk", lambda i: (i + 4) % 8, 8)


def by_head(*rows):
    stacked = jnp.concatenate([r.reshape(T, U, 1, W) for r in rows], axis=2)
    return jnp.transpose(stacked, (1, 2, 0, 3))


def exchange(x):
    return lax.all_to_all(x, "uly", split_axis=0, concat_axis=0, tiled=True)


def to_tokens(x):
    got = exchange(x)
    return [jnp.transpose(got[:, i], (1, 0, 2)).reshape(T, U * W) for i in range(x.shape[1])]


def after(x, *others):
    return lax.optimization_barrier((x, *others))[0]


def per_device(query_rows, key_rows, value_rows, out_grad, out_weight):
    uly, blk = lax.axis_index("uly"), lax.axis_index("blk")
    place = jnp.stack([uly // 2, uly % 2, lax.axis_index("dp") * 2 + blk // 4, blk % 4]).astype(jnp.int32)
    leaving = by_head(key_rows, value_rows, query_rows)
    grad_block = lax.all_gather(out_grad, "uly", axis=0, tiled=True)
    shards = (out_weight, y_shift(out_weight, -1), y_shift(out_weight, 2), y_shift(out_weight, 1))
    heads = exchange(leaving)
    weight_own = stacked_rows(*after(shards, leaving))
    heads = after(heads, weight_own)
    kv0, qa = heads[:, :2], heads[:, 2]
    kv_prev, kv_next = y_shift(kv0, 1), y_shift(kv0, -1)
    qb = z_swap(qa)
    weight_below, weight_above = z_shift(weight_own, 1), z_shift(weight_own, -1)
    cut = QUARTER // 2
    weights = (weight_own, weight_above, z_shift(weight_above[:cut], -1), z_shift(weight_below[cut:], 1), weight_below)
    far_low, far_high = y_shift(kv_prev[: U // 2], 1), y_shift(kv_next[U // 2 :], -1)
    ot, st = forward_near(qa, qb, kv0, kv_prev, kv_next)
    da = project(after(place, ot), grad_block, weights)
    db = z_swap(da)
    ot, st = forward_far(after(qa, da), qb, far_low, far_high, ot, st)
    st = row_dots(ot, st, da, db)
    o_keep, o_send, fin = merge(ot, st, z_swap(st))
    attn_out = (o_keep + z_swap(o_send).astype(F32)).astype(BF)
    common = (qa, qb, da, db, fin)

    low, high, dqt = backward_far(common, far_low, far_high)
    low_got, high_got = y_shift(low, 1), y_shift(high, -1)
    half = struct((QUARTER // 2, W), BF)
    a, b = weight_call(weight_far_kernel, "weight_far", 1, [half, half], [], place, grad_block, after(attn_out, dqt))
    a_got, b_got = z_shift(a, 1), z_shift(b, -1)
    g_prev, g_next, dqt = backward_near(common, kv_prev, kv_next, after(dqt, a, b))
    low_half, high_half = slice(0, U // 2), slice(U // 2, U)
    to_next = jnp.concatenate([g_next[low_half] + low_got.astype(F32), g_next[high_half]], axis=0)
    to_prev = jnp.concatenate([g_prev[low_half], g_prev[high_half] + high_got.astype(F32)], axis=0)
    from_below, from_above = y_shift(to_next.astype(BF), 1), y_shift(to_prev.astype(BF), -1)
    g_own, q_keep, q_send = backward_own(common, kv0, dqt)
    whole = struct((QUARTER, W), BF)
    up, down = weight_call(
        weight_near_kernel, "weight_near", 2, [whole, whole], [], place, grad_block, after(attn_out, q_send), a_got, b_got
    )
    below, above = z_shift(up, 1), z_shift(down, -1)
    dq = (q_keep + z_swap(q_send).astype(F32)).astype(BF)
    dkv = (g_own + from_below.astype(F32) + from_above.astype(F32)).astype(BF)
    grads = jnp.concatenate([dkv, dq[:, None]], axis=1)
    grad_key, grad_value, grad_query = to_tokens(grads)
    o0, o1, o2, o3 = weight_call(
        weight_own_kernel,
        "weight_own",
        1,
        [struct((SHARD, W), F32)] + [struct((SHARD, W), BF)] * 3,
        [pltpu.VMEM((QUARTER, W), F32)],
        place,
        grad_block,
        after(attn_out, grads),
        below,
        above,
    )
    grad_weight = o0 + y_shift(o1, 1).astype(F32) + y_shift(o2, 2).astype(F32) + y_shift(o3, -1).astype(F32)
    return (grad_query, grad_key, grad_value, grad_weight)


def solution(mesh):
    rows = P(("dp", "blk", "uly"), None)
    weight = P(("dp", "blk"), "uly")
    return jax.shard_map(
        per_device,
        mesh=mesh,
        in_specs=(rows, rows, rows, rows, weight),
        out_specs=(rows, rows, rows, weight),
        check_vma=False,
    )
```

```python
import functools

import jax
import jax.numpy as jnp
from jax import lax
from jax.experimental import pallas as pl
from jax.experimental.pallas import tpu as pltpu
from jax.sharding import PartitionSpec as P

HD = 128
HEADS = 3
U = 8
T = 64
W = HEADS * HD
ROWS = U * T
SCALE = HD**-0.5
SCALE2 = SCALE * 1.4426950408889634
BF = jnp.bfloat16
F32 = jnp.float32
VMEM = 60 * 1024 * 1024


def nt(a, b):
    return lax.dot_general(a, b, (((1,), (1,)), ((), ())), preferred_element_type=F32)


def nn(a, b):
    return jnp.dot(a, b, preferred_element_type=F32)


def flat(ref):
    return ref[...].reshape(ROWS, HD)


def forward_blocks(queries, blocks, state):
    top, total, acc = state
    later = nt(blocks[0][0], queries)
    for j, (_, values) in enumerate(blocks):
        scores = later
        if j + 1 < len(blocks):
            later = nt(blocks[j + 1][0], queries)
        peak = jnp.max(scores, axis=0, keepdims=True) * SCALE2
        if top is not None:
            peak = jnp.maximum(peak, top)
        weights = jnp.exp2(scores * SCALE2 - peak)
        sums = jnp.sum(weights, axis=0, keepdims=True)
        out = nn(values.T, weights.astype(BF))
        if top is not None:
            fade = jnp.exp2(top - peak)
            sums = sums + total * fade
            out = out + acc * fade
        top, total, acc = peak, sums, out
    return top, total, acc


def forward_near_kernel(qa, qb, kv0, kv1, kv2, ot_ref, st_ref):
    queries = jnp.concatenate([flat(qa), flat(qb)], axis=0)
    blocks = [(r[:, 0].reshape(ROWS, HD), r[:, 1].reshape(ROWS, HD)) for r in (kv0, kv1, kv2)]
    st_ref[0, 0:1], st_ref[0, 1:2], ot_ref[...] = forward_blocks(queries, blocks, (None, None, None))


def forward_far_kernel(qa, qb, kv3, ot_in, st_in, ot_ref, st_ref):
    queries = jnp.concatenate([flat(qa), flat(qb)], axis=0)
    blocks = [(kv3[:, 0].reshape(ROWS, HD), kv3[:, 1].reshape(ROWS, HD))]
    state = (st_in[0, 0:1], st_in[0, 1:2], ot_in[...])
    st_ref[0, 0:1], st_ref[0, 1:2], ot_ref[...] = forward_blocks(queries, blocks, state)


Q_SPEC = pl.BlockSpec((U, T, HD), lambda h: (0, 0, h))
KV_SPEC = pl.BlockSpec((U, 2, T, HD), lambda h: (0, 0, 0, h))
HALF_SPEC = pl.BlockSpec((U // 2, 2, T, HD), lambda h: (0, 0, 0, h))
OT_SPEC = pl.BlockSpec((HD, 2 * ROWS), lambda h: (h, 0))
ST_SPEC = pl.BlockSpec((1, 8, 2 * ROWS), lambda h: (h, 0, 0))
ROW_SPEC = pl.BlockSpec((ROWS, HD), lambda h: (0, h))
SMALL_VMEM = 24 * 1024 * 1024
PARAMS = pltpu.CompilerParams(vmem_limit_bytes=VMEM, dimension_semantics=("arbitrary",))
SMALL = pltpu.CompilerParams(vmem_limit_bytes=SMALL_VMEM, dimension_semantics=("arbitrary",))


def struct(shape, dtype):
    return jax.ShapeDtypeStruct(shape, dtype)


def cost(flops, nbytes):
    return pl.CostEstimate(flops=flops, bytes_accessed=nbytes, transcendentals=0)


def forward_call(kernel, name, blocks, in_specs, operands):
    return pl.pallas_call(
        kernel,
        grid=(HEADS,),
        in_specs=in_specs,
        out_specs=[OT_SPEC, ST_SPEC],
        out_shape=[struct((W, 2 * ROWS), F32), struct((HEADS, 8, 2 * ROWS), F32)],
        compiler_params=PARAMS,
        cost_estimate=cost(blocks * 4 * 1024 * ROWS * W, (blocks + 2) << 20),
        name=name,
    )(*operands)


def forward_near(*operands):
    return forward_call(forward_near_kernel, "forward_near", 3, [Q_SPEC] * 2 + [KV_SPEC] * 3, operands)


def forward_far(*operands):
    specs = [Q_SPEC] * 2 + [KV_SPEC, OT_SPEC, ST_SPEC]
    return forward_call(forward_far_kernel, "forward_far", 1, specs, operands)


def dot_kernel(ot_ref, st_ref, da, db, out_ref):
    out_ref[0, 0:2] = st_ref[0, 0:2]
    for part, d in enumerate((da, db)):
        at = slice(part * ROWS, (part + 1) * ROWS)
        grad_t = d[...].astype(F32).T
        out_ref[0, 2:3, at] = jnp.sum(grad_t * ot_ref[:, at], axis=0, keepdims=True)


def row_dots(ot, st, da, db):
    return pl.pallas_call(
        dot_kernel,
        grid=(HEADS,),
        in_specs=[OT_SPEC, ST_SPEC, ROW_SPEC, ROW_SPEC],
        out_specs=ST_SPEC,
        out_shape=struct((HEADS, 8, 2 * ROWS), F32),
        compiler_params=SMALL,
        cost_estimate=cost(1 << 20, 3 << 20),
        name="row_dots",
    )(ot, st, da, db)


def merge_kernel(ot_ref, st_ref, pst_ref, keep_ref, send_ref, fin_ref):
    mine = st_ref[0]
    other = pst_ref[0]
    other = jnp.concatenate([other[:, ROWS:], other[:, :ROWS]], axis=1)
    top = jnp.maximum(mine[0:1], other[0:1])
    a = jnp.exp2(mine[0:1] - top)
    b = jnp.exp2(other[0:1] - top)
    total = a * mine[1:2] + b * other[1:2]
    fin_ref[0, 0:1] = top + jnp.log2(total)
    fin_ref[0, 1:2] = (a * mine[2:3] + b * other[2:3]) / total
    out_t = ot_ref[...] * (a / total)
    keep_ref[...] = out_t[:, :ROWS].T
    send_ref[...] = out_t[:, ROWS:].T.astype(BF)


def merge(ot, st, pst):
    return pl.pallas_call(
        merge_kernel,
        grid=(HEADS,),
        in_specs=[OT_SPEC, ST_SPEC, ST_SPEC],
        out_specs=[ROW_SPEC, ROW_SPEC, ST_SPEC],
        out_shape=[struct((ROWS, W), F32), struct((ROWS, W), BF), struct((HEADS, 8, 2 * ROWS), F32)],
        compiler_params=SMALL,
        cost_estimate=cost(1 << 20, 3 << 20),
        name="merge_halves",
    )(ot, st, pst)


FEATURES = 5120
QUARTER = FEATURES // 4
SHARD = FEATURES // 16
ANY_SPEC = pl.BlockSpec(memory_space=pl.ANY)
SMEM_SPEC = pl.BlockSpec(memory_space=pltpu.SMEM)
VMEM_SPEC = pl.BlockSpec(memory_space=pltpu.VMEM)
PLAIN = pltpu.CompilerParams(vmem_limit_bytes=VMEM)


def stack_kernel(*refs):
    for i, piece in enumerate(refs[:4]):
        refs[4][i * SHARD : (i + 1) * SHARD] = piece[...]


def stacked_rows(*pieces):
    return pl.pallas_call(
        stack_kernel,
        in_specs=[VMEM_SPEC] * 4,
        out_specs=VMEM_SPEC,
        out_shape=struct((QUARTER, W), BF),
        compiler_params=pltpu.CompilerParams(vmem_limit_bytes=SMALL_VMEM),
        cost_estimate=cost(0, 2 << 20),
        name="stack_rows",
    )(*pieces)


def project_kernel(place, grad, w0, w1, w2a, w2b, w3, out_ref, held, weight, sems):
    groups = []
    for oz in range(4):
        quarter = lax.rem(place[2] + oz, 4)
        columns = pl.ds(pl.multiple_of(quarter * QUARTER, 128), QUARTER)
        copies = [pltpu.make_async_copy(grad.at[:, columns], held.at[oz], sems.at[oz, 4])]
        for oy in range(4):
            source, row = ((w0, oy), (w1, oy), (w2a, oy) if oy < 2 else (w2b, oy - 2), (w3, oy))[oz]
            at = pl.multiple_of(lax.rem(place[3] + oy, 4) * SHARD, SHARD)
            target = weight.at[oz, pl.ds(at, SHARD)]
            copies.append(pltpu.make_async_copy(source.at[pl.ds(row * SHARD, SHARD)], target, sems.at[oz, oy]))
        for c in copies:
            c.start()
        groups.append(copies)
    total = None
    for oz in range(4):
        for c in groups[oz]:
            c.wait()
        part = nn(held[oz], weight[oz])
        total = part if total is None else total + part
    out_ref[...] = total.astype(BF)


def project(place, grad, weights):
    return pl.pallas_call(
        project_kernel,
        in_specs=[SMEM_SPEC] + [ANY_SPEC] * 6,
        out_specs=VMEM_SPEC,
        out_shape=struct((ROWS, W), BF),
        scratch_shapes=[
            pltpu.VMEM((4, ROWS, QUARTER), BF),
            pltpu.VMEM((4, QUARTER, W), BF),
            pltpu.SemaphoreType.DMA((4, 5)),
        ],
        compiler_params=PLAIN,
        cost_estimate=cost(2 * ROWS * FEATURES * W, 10 << 20),
        name="project",
    )(place, grad, *weights)


def tn(a, b):
    return lax.dot_general(a, b, (((0,), (0,)), ((), ())), preferred_element_type=F32)


def weight_part(place, oz, grad, attn, held, sem):
    at = lax.rem(place[2] + oz, 4) * QUARTER
    copy = pltpu.make_async_copy(grad.at[:, pl.ds(pl.multiple_of(at, 128), QUARTER)], held, sem)
    copy.start()
    copy.wait()
    return tn(held[...], attn[...])


def weight_far_kernel(place, grad, keep, got, a_ref, b_ref, attn_ref, held, sem):
    attn_ref[...] = (keep[...] + got[...].astype(F32)).astype(BF)
    part = weight_part(place, 2, grad, attn_ref, held, sem).astype(BF)
    a_ref[...] = part[: QUARTER // 2]
    b_ref[...] = part[QUARTER // 2 :]


def weight_near_kernel(place, grad, attn, a_got, b_got, up_ref, down_ref, held, sem):
    half = QUARTER // 2
    part = weight_part(place, 1, grad, attn, held, sem)
    up_ref[:half] = (part[:half] + a_got[...].astype(F32)).astype(BF)
    up_ref[half:] = part[half:].astype(BF)
    part = weight_part(place, 3, grad, attn, held, sem)
    down_ref[:half] = part[:half].astype(BF)
    down_ref[half:] = (part[half:] + b_got[...].astype(F32)).astype(BF)


def weight_own_kernel(place, grad, attn, out_ref, held, sem):
    out_ref[...] = weight_part(place, 0, grad, attn, held, sem)


def weight_sum_kernel(place, mine, below, above, o0, o1, o2, o3):
    for oy, o in enumerate((o0, o1, o2, o3)):
        rows = pl.ds(pl.multiple_of(lax.rem(place[3] + oy, 4) * SHARD, SHARD), SHARD)
        o[...] = (mine[rows] + below[rows].astype(F32) + above[rows].astype(F32)).astype(o.dtype)


def weight_sum(place, mine, below, above):
    return pl.pallas_call(
        weight_sum_kernel,
        in_specs=[SMEM_SPEC] + [VMEM_SPEC] * 3,
        out_specs=[VMEM_SPEC] * 4,
        out_shape=[struct((SHARD, W), F32)] + [struct((SHARD, W), BF)] * 3,
        compiler_params=PLAIN,
        cost_estimate=cost(1 << 20, 5 << 20),
        name="weight_sum",
    )(place, mine, below, above)


def weight_call(kernel, name, parts, outs, extra, place, grad, *more):
    return pl.pallas_call(
        kernel,
        in_specs=[SMEM_SPEC, ANY_SPEC] + [VMEM_SPEC] * len(more),
        out_specs=[VMEM_SPEC] * len(outs),
        out_shape=outs,
        scratch_shapes=[pltpu.VMEM((ROWS, QUARTER), BF), pltpu.SemaphoreType.DMA] + extra,
        compiler_params=PLAIN,
        cost_estimate=cost(parts * 2 * ROWS * QUARTER * W, parts * 3 << 20),
        name=name,
    )(place, grad, *more)


CHUNK = 256


def backward_block(keys, values, queries, grads, log_total, row_dot):
    scores = nt(keys, queries)
    probs = jnp.exp2(scores * SCALE2 - log_total)
    grad_probs = nt(values, grads)
    grad_scores = (probs * (grad_probs - row_dot)).astype(BF)
    grad_values = nn(probs.astype(BF), grads)
    grad_keys = nn(grad_scores, queries) * SCALE
    grad_queries_t = nn(keys.T, grad_scores)
    return grad_keys, grad_values, grad_queries_t


def backward_common(qa, qb, da, db, fin):
    queries = jnp.concatenate([flat(qa), flat(qb)], axis=0)
    grads = jnp.concatenate([da[...], db[...]], axis=0)
    return queries, grads, fin[0, 0:1], fin[0, 1:2]


def chunks_of(x):
    return [x[i * CHUNK : (i + 1) * CHUNK] for i in range(ROWS // CHUNK)]


def run_block(keys, values, common):
    dks, dvs, dqt = [], [], None
    for k, v in zip(chunks_of(keys), chunks_of(values)):
        dk, dv, q = backward_block(k, v, *common)
        dks.append(dk)
        dvs.append(dv)
        dqt = q if dqt is None else dqt + q
    return jnp.concatenate(dks, axis=0), jnp.concatenate(dvs, axis=0), dqt


def store_halves(low, high, i, x):
    low[:, i] = x[: ROWS // 2].astype(low.dtype).reshape(U // 2, T, HD)
    high[:, i] = x[ROWS // 2 :].astype(high.dtype).reshape(U // 2, T, HD)


def far_kernel(qa, qb, da, db, fin, kv3, low_ref, high_ref, dqt_ref):
    common = backward_common(qa, qb, da, db, fin)
    dk, dv, dqt = run_block(kv3[:, 0].reshape(ROWS, HD), kv3[:, 1].reshape(ROWS, HD), common)
    store_halves(low_ref, high_ref, 0, dk)
    store_halves(low_ref, high_ref, 1, dv)
    dqt_ref[...] = dqt


def store_sum(o, i, x, got, first):
    half = ROWS // 2
    at = slice(first, first + half)
    rest = slice(half - first, ROWS - first)
    u, r = slice(first // T, (first + half) // T), slice((half - first) // T, (ROWS - first) // T)
    o[u, i] = (x[at] + got[:, i].reshape(half, HD).astype(F32)).astype(BF).reshape(U // 2, T, HD)
    o[r, i] = x[rest].astype(BF).reshape(U // 2, T, HD)


def near_kernel(qa, qb, da, db, fin, kv1, kv2, dqt_in, low, high, o1_ref, o2_ref, dqt_ref):
    common = backward_common(qa, qb, da, db, fin)
    total = dqt_in[...]
    for kv, o, got, first in ((kv1, o1_ref, high, ROWS // 2), (kv2, o2_ref, low, 0)):
        dk, dv, dqt = run_block(kv[:, 0].reshape(ROWS, HD), kv[:, 1].reshape(ROWS, HD), common)
        store_sum(o, 0, dk, got, first)
        store_sum(o, 1, dv, got, first)
        total = total + dqt
    dqt_ref[...] = total


def own_kernel(qa, qb, da, db, fin, kv0, dqt_in, o0_ref, qkeep_ref, qsend_ref):
    common = backward_common(qa, qb, da, db, fin)
    dk, dv, dqt = run_block(kv0[:, 0].reshape(ROWS, HD), kv0[:, 1].reshape(ROWS, HD), common)
    o0_ref[:, 0] = dk.reshape(U, T, HD)
    o0_ref[:, 1] = dv.reshape(U, T, HD)
    total = (dqt_in[...] + dqt) * SCALE
    qkeep_ref[...] = total[:, :ROWS].T.reshape(U, T, HD)
    qsend_ref[...] = total[:, ROWS:].T.astype(BF).reshape(U, T, HD)


COMMON_SPECS = [Q_SPEC, Q_SPEC, ROW_SPEC, ROW_SPEC, ST_SPEC]


def backward_far(common, kv3):
    return pl.pallas_call(
        far_kernel,
        grid=(HEADS,),
        in_specs=COMMON_SPECS + [KV_SPEC],
        out_specs=[HALF_SPEC, HALF_SPEC, OT_SPEC],
        out_shape=[struct((U // 2, 2, T, W), BF)] * 2 + [struct((W, 2 * ROWS), F32)],
        compiler_params=PARAMS,
        cost_estimate=cost(5 * 2 * 1024 * 512 * W, 6 << 20),
        name="backward_far",
    )(*common, kv3)


def backward_near(common, kv1, kv2, dqt, low, high):
    return pl.pallas_call(
        near_kernel,
        grid=(HEADS,),
        in_specs=COMMON_SPECS + [KV_SPEC, KV_SPEC, OT_SPEC, HALF_SPEC, HALF_SPEC],
        out_specs=[KV_SPEC, KV_SPEC, OT_SPEC],
        out_shape=[struct((U, 2, T, W), BF)] * 2 + [struct((W, 2 * ROWS), F32)],
        compiler_params=PARAMS,
        cost_estimate=cost(5 * 2 * 1024 * 1024 * W, 9 << 20),
        name="backward_near",
    )(*common, kv1, kv2, dqt, low, high)


def backward_own(common, kv0, dqt):
    return pl.pallas_call(
        own_kernel,
        grid=(HEADS,),
        in_specs=COMMON_SPECS + [KV_SPEC, OT_SPEC],
        out_specs=[KV_SPEC, Q_SPEC, Q_SPEC],
        out_shape=[struct((U, 2, T, W), F32), struct((U, T, W), F32), struct((U, T, W), BF)],
        compiler_params=PARAMS,
        cost_estimate=cost(5 * 2 * 1024 * 512 * W, 8 << 20),
        name="backward_own",
    )(*common, kv0, dqt)


def move(x, axis, to, n):
    return lax.ppermute(x, axis, [(i, to(i)) for i in range(n)])


def y_shift(x, d):
    return move(x, "blk", lambda i: i // 4 * 4 + (i + d) % 4, 8)


def z_shift(x, d):
    return move(x, ("dp", "blk"), lambda i: (i // 4 + d) % 4 * 4 + i % 4, 16)


def z_swap(x):
    return move(x, "blk", lambda i: (i + 4) % 8, 8)


def by_head(*rows):
    stacked = jnp.concatenate([r.reshape(T, U, 1, W) for r in rows], axis=2)
    return jnp.transpose(stacked, (1, 2, 0, 3))


def exchange(x):
    return lax.all_to_all(x, "uly", split_axis=0, concat_axis=0, tiled=True)


def to_tokens(x):
    got = exchange(x)
    return [jnp.transpose(got[:, i], (1, 0, 2)).reshape(T, U * W) for i in range(x.shape[1])]


def after(x, *others):
    return lax.optimization_barrier((x, *others))[0]


def per_device(query_rows, key_rows, value_rows, out_grad, out_weight):
    uly, blk = lax.axis_index("uly"), lax.axis_index("blk")
    place = jnp.stack([uly // 2, uly % 2, lax.axis_index("dp") * 2 + blk // 4, blk % 4]).astype(jnp.int32)
    leaving = by_head(key_rows, value_rows, query_rows)
    grad_block = lax.all_gather(out_grad, "uly", axis=0, tiled=True)
    shards = (out_weight, y_shift(out_weight, -1), y_shift(out_weight, 2), y_shift(out_weight, 1))
    heads = exchange(leaving)
    shards, place = after((shards, place), leaving)
    weight_own = stacked_rows(*shards)
    heads = after(heads, weight_own)
    kv0, qa = heads[:, :2], heads[:, 2]
    kv_prev, kv_next = y_shift(kv0, 1), y_shift(kv0, -1)
    qb = z_swap(qa)
    weight_below, weight_above = z_shift(weight_own, 1), z_shift(weight_own, -1)
    cut = QUARTER // 2
    weights = (weight_own, weight_above, z_shift(weight_above[:cut], -1), z_shift(weight_below[cut:], 1), weight_below)
    kv_far = y_shift(kv_prev, 1)
    ot, st = forward_near(qa, qb, kv0, kv_prev, kv_next)
    da = project(after(place, ot), grad_block, weights)
    db = z_swap(da)
    ot, st = forward_far(after(qa, da), qb, kv_far, ot, st)
    st = row_dots(ot, st, da, db)
    o_keep, o_send, fin = merge(ot, st, z_swap(st))
    o_got = z_swap(o_send)
    common = (qa, qb, da, db, fin)

    low, high, dqt = backward_far(common, kv_far)
    low_got, high_got = y_shift(low, 1), y_shift(high, -1)
    half = struct((QUARTER // 2, W), BF)
    outs = [half, half, struct((ROWS, W), BF)]
    a, b, attn_out = weight_call(weight_far_kernel, "weight_far", 1, outs, [], place, grad_block, after(o_keep, dqt), o_got)
    a_got, b_got = z_shift(a, 1), z_shift(b, -1)
    to_prev, to_next, dqt = backward_near(common, kv_prev, kv_next, after(dqt, a, b), low_got, high_got)
    from_below, from_above = y_shift(to_next, 1), y_shift(to_prev, -1)
    g_own, q_keep, q_send = backward_own(common, kv0, dqt)
    whole = struct((QUARTER, W), BF)
    up, down = weight_call(
        weight_near_kernel, "weight_near", 2, [whole, whole], [], place, grad_block, after(attn_out, q_send), a_got, b_got
    )
    below, above = z_shift(up, 1), z_shift(down, -1)
    dq = (after(q_keep, up) + z_swap(q_send).astype(F32)).astype(BF)
    dkv = (g_own + from_below.astype(F32) + from_above.astype(F32)).astype(BF)
    grads = jnp.concatenate([dkv, dq[:, None]], axis=1)
    grad_key, grad_value, grad_query = to_tokens(grads)
    outs = [struct((QUARTER, W), F32)]
    (mine,) = weight_call(weight_own_kernel, "weight_own", 1, outs, [], place, grad_block, after(attn_out, grads))
    o0, o1, o2, o3 = weight_sum(place, mine, below, above)
    grad_weight = o0 + y_shift(o1, 1).astype(F32) + y_shift(o2, 2).astype(F32) + y_shift(o3, -1).astype(F32)
    return (grad_query, grad_key, grad_value, grad_weight)


def solution(mesh):
    rows = P(("dp", "blk", "uly"), None)
    weight = P(("dp", "blk"), "uly")
    return jax.shard_map(
        per_device,
        mesh=mesh,
        in_specs=(rows, rows, rows, rows, weight),
        out_specs=(rows, rows, rows, weight),
        check_vma=False,
    )
```

```python
import functools

import jax
import jax.numpy as jnp
from jax import lax
from jax.experimental import pallas as pl
from jax.experimental.pallas import tpu as pltpu
from jax.sharding import PartitionSpec as P

HD = 128
HEADS = 3
U = 8
T = 64
W = HEADS * HD
ROWS = U * T
SCALE = HD**-0.5
SCALE2 = SCALE * 1.4426950408889634
BF = jnp.bfloat16
F32 = jnp.float32
VMEM = 60 * 1024 * 1024


def nt(a, b):
    return lax.dot_general(a, b, (((1,), (1,)), ((), ())), preferred_element_type=F32)


def nn(a, b):
    return jnp.dot(a, b, preferred_element_type=F32)


def flat(ref):
    return ref[...].reshape(ROWS, HD)


def forward_blocks(queries, blocks, state):
    top, total, acc = state
    later = nt(blocks[0][0], queries)
    for j, (_, values) in enumerate(blocks):
        scores = later
        if j + 1 < len(blocks):
            later = nt(blocks[j + 1][0], queries)
        peak = jnp.max(scores, axis=0, keepdims=True) * SCALE2
        if top is not None:
            peak = jnp.maximum(peak, top)
        weights = jnp.exp2(scores * SCALE2 - peak)
        sums = jnp.sum(weights, axis=0, keepdims=True)
        out = nn(values.T, weights.astype(BF))
        if top is not None:
            fade = jnp.exp2(top - peak)
            sums = sums + total * fade
            out = out + acc * fade
        top, total, acc = peak, sums, out
    return top, total, acc


def forward_near_kernel(qa, qb, kv0, kv1, kv2, ot_ref, st_ref):
    queries = jnp.concatenate([flat(qa), flat(qb)], axis=0)
    blocks = [(r[:, 0].reshape(ROWS, HD), r[:, 1].reshape(ROWS, HD)) for r in (kv0, kv1, kv2)]
    st_ref[0, 0:1], st_ref[0, 1:2], ot_ref[...] = forward_blocks(queries, blocks, (None, None, None))


def forward_far_kernel(qa, qb, kv3, ot_in, st_in, ot_ref, st_ref):
    queries = jnp.concatenate([flat(qa), flat(qb)], axis=0)
    blocks = [(kv3[:, 0].reshape(ROWS, HD), kv3[:, 1].reshape(ROWS, HD))]
    state = (st_in[0, 0:1], st_in[0, 1:2], ot_in[...])
    st_ref[0, 0:1], st_ref[0, 1:2], ot_ref[...] = forward_blocks(queries, blocks, state)


Q_SPEC = pl.BlockSpec((U, T, HD), lambda h: (0, 0, h))
KV_SPEC = pl.BlockSpec((U, 2, T, HD), lambda h: (0, 0, 0, h))
HALF_SPEC = pl.BlockSpec((U // 2, 2, T, HD), lambda h: (0, 0, 0, h))
OT_SPEC = pl.BlockSpec((HD, 2 * ROWS), lambda h: (h, 0))
ST_SPEC = pl.BlockSpec((1, 8, 2 * ROWS), lambda h: (h, 0, 0))
ROW_SPEC = pl.BlockSpec((ROWS, HD), lambda h: (0, h))
SMALL_VMEM = 24 * 1024 * 1024
PARAMS = pltpu.CompilerParams(vmem_limit_bytes=VMEM, dimension_semantics=("arbitrary",))
SMALL = pltpu.CompilerParams(vmem_limit_bytes=SMALL_VMEM, dimension_semantics=("arbitrary",))


def struct(shape, dtype):
    return jax.ShapeDtypeStruct(shape, dtype)


def cost(flops, nbytes):
    return pl.CostEstimate(flops=flops, bytes_accessed=nbytes, transcendentals=0)


def forward_call(kernel, name, blocks, in_specs, operands):
    return pl.pallas_call(
        kernel,
        grid=(HEADS,),
        in_specs=in_specs,
        out_specs=[OT_SPEC, ST_SPEC],
        out_shape=[struct((W, 2 * ROWS), F32), struct((HEADS, 8, 2 * ROWS), F32)],
        compiler_params=PARAMS,
        cost_estimate=cost(blocks * 4 * 1024 * ROWS * W, (blocks + 2) << 20),
        name=name,
    )(*operands)


def forward_near(*operands):
    return forward_call(forward_near_kernel, "forward_near", 3, [Q_SPEC] * 2 + [KV_SPEC] * 3, operands)


def forward_far(*operands):
    specs = [Q_SPEC] * 2 + [KV_SPEC, OT_SPEC, ST_SPEC]
    return forward_call(forward_far_kernel, "forward_far", 1, specs, operands)


def dot_kernel(ot_ref, st_ref, da, db, out_ref):
    out_ref[0, 0:2] = st_ref[0, 0:2]
    for part, d in enumerate((da, db)):
        at = slice(part * ROWS, (part + 1) * ROWS)
        grad_t = d[...].astype(F32).T
        out_ref[0, 2:3, at] = jnp.sum(grad_t * ot_ref[:, at], axis=0, keepdims=True)


def row_dots(ot, st, da, db):
    return pl.pallas_call(
        dot_kernel,
        grid=(HEADS,),
        in_specs=[OT_SPEC, ST_SPEC, ROW_SPEC, ROW_SPEC],
        out_specs=ST_SPEC,
        out_shape=struct((HEADS, 8, 2 * ROWS), F32),
        compiler_params=SMALL,
        cost_estimate=cost(1 << 20, 3 << 20),
        name="row_dots",
    )(ot, st, da, db)


def merge_kernel(ot_ref, st_ref, pst_ref, keep_ref, send_ref, fin_ref):
    mine = st_ref[0]
    other = pst_ref[0]
    other = jnp.concatenate([other[:, ROWS:], other[:, :ROWS]], axis=1)
    top = jnp.maximum(mine[0:1], other[0:1])
    a = jnp.exp2(mine[0:1] - top)
    b = jnp.exp2(other[0:1] - top)
    total = a * mine[1:2] + b * other[1:2]
    fin_ref[0, 0:1] = top + jnp.log2(total)
    fin_ref[0, 1:2] = (a * mine[2:3] + b * other[2:3]) / total
    out_t = ot_ref[...] * (a / total)
    keep_ref[...] = out_t[:, :ROWS].T
    send_ref[...] = out_t[:, ROWS:].T.astype(BF)


def merge(ot, st, pst):
    return pl.pallas_call(
        merge_kernel,
        grid=(HEADS,),
        in_specs=[OT_SPEC, ST_SPEC, ST_SPEC],
        out_specs=[ROW_SPEC, ROW_SPEC, ST_SPEC],
        out_shape=[struct((ROWS, W), F32), struct((ROWS, W), BF), struct((HEADS, 8, 2 * ROWS), F32)],
        compiler_params=SMALL,
        cost_estimate=cost(1 << 20, 3 << 20),
        name="merge_halves",
    )(ot, st, pst)


FEATURES = 5120
QUARTER = FEATURES // 4
SHARD = FEATURES // 16
ANY_SPEC = pl.BlockSpec(memory_space=pl.ANY)
SMEM_SPEC = pl.BlockSpec(memory_space=pltpu.SMEM)
VMEM_SPEC = pl.BlockSpec(memory_space=pltpu.VMEM)
PLAIN = pltpu.CompilerParams(vmem_limit_bytes=VMEM)


def stack_kernel(*refs):
    for i, piece in enumerate(refs[:4]):
        refs[4][i * SHARD : (i + 1) * SHARD] = piece[...]


def stacked_rows(*pieces):
    return pl.pallas_call(
        stack_kernel,
        in_specs=[VMEM_SPEC] * 4,
        out_specs=VMEM_SPEC,
        out_shape=struct((QUARTER, W), BF),
        compiler_params=pltpu.CompilerParams(vmem_limit_bytes=SMALL_VMEM),
        cost_estimate=cost(0, 2 << 20),
        name="stack_rows",
    )(*pieces)


def project_kernel(place, grad, w0, w1, w2a, w2b, w3, out_ref, held, weight, sems):
    groups = []
    for oz in range(4):
        quarter = lax.rem(place[2] + oz, 4)
        columns = pl.ds(pl.multiple_of(quarter * QUARTER, 128), QUARTER)
        copies = [pltpu.make_async_copy(grad.at[:, columns], held.at[oz], sems.at[oz, 4])]
        for oy in range(4):
            source, row = ((w0, oy), (w1, oy), (w2a, oy) if oy < 2 else (w2b, oy - 2), (w3, oy))[oz]
            at = pl.multiple_of(lax.rem(place[3] + oy, 4) * SHARD, SHARD)
            target = weight.at[oz, pl.ds(at, SHARD)]
            copies.append(pltpu.make_async_copy(source.at[pl.ds(row * SHARD, SHARD)], target, sems.at[oz, oy]))
        for c in copies:
            c.start()
        groups.append(copies)
    total = None
    for oz in range(4):
        for c in groups[oz]:
            c.wait()
        part = nn(held[oz], weight[oz])
        total = part if total is None else total + part
    out_ref[...] = total.astype(BF)


def project(place, grad, weights):
    return pl.pallas_call(
        project_kernel,
        in_specs=[SMEM_SPEC] + [ANY_SPEC] * 6,
        out_specs=VMEM_SPEC,
        out_shape=struct((ROWS, W), BF),
        scratch_shapes=[
            pltpu.VMEM((4, ROWS, QUARTER), BF),
            pltpu.VMEM((4, QUARTER, W), BF),
            pltpu.SemaphoreType.DMA((4, 5)),
        ],
        compiler_params=PLAIN,
        cost_estimate=cost(2 * ROWS * FEATURES * W, 10 << 20),
        name="project",
    )(place, grad, *weights)


def tn(a, b):
    return lax.dot_general(a, b, (((0,), (0,)), ((), ())), preferred_element_type=F32)


def weight_part(place, oz, grad, attn, held, sem):
    at = lax.rem(place[2] + oz, 4) * QUARTER
    copy = pltpu.make_async_copy(grad.at[:, pl.ds(pl.multiple_of(at, 128), QUARTER)], held, sem)
    copy.start()
    copy.wait()
    return tn(held[...], attn[...])


def weight_far_kernel(place, grad, attn, a_ref, b_ref, held, sem):
    part = weight_part(place, 2, grad, attn, held, sem).astype(BF)
    a_ref[...] = part[: QUARTER // 2]
    b_ref[...] = part[QUARTER // 2 :]


def weight_near_kernel(place, grad, attn, a_got, b_got, up_ref, down_ref, held, sem):
    half = QUARTER // 2
    part = weight_part(place, 1, grad, attn, held, sem)
    up_ref[:half] = (part[:half] + a_got[...].astype(F32)).astype(BF)
    up_ref[half:] = part[half:].astype(BF)
    part = weight_part(place, 3, grad, attn, held, sem)
    down_ref[:half] = part[:half].astype(BF)
    down_ref[half:] = (part[half:] + b_got[...].astype(F32)).astype(BF)


def weight_own_kernel(place, grad, attn, out_ref, held, sem):
    out_ref[...] = weight_part(place, 0, grad, attn, held, sem)


def weight_sum_kernel(place, mine, below, above, o0, o1, o2, o3):
    for oy, o in enumerate((o0, o1, o2, o3)):
        rows = pl.ds(pl.multiple_of(lax.rem(place[3] + oy, 4) * SHARD, SHARD), SHARD)
        o[...] = (mine[rows] + below[rows].astype(F32) + above[rows].astype(F32)).astype(o.dtype)


def weight_sum(place, mine, below, above):
    return pl.pallas_call(
        weight_sum_kernel,
        in_specs=[SMEM_SPEC] + [VMEM_SPEC] * 3,
        out_specs=[VMEM_SPEC] * 4,
        out_shape=[struct((SHARD, W), F32)] + [struct((SHARD, W), BF)] * 3,
        compiler_params=PLAIN,
        cost_estimate=cost(1 << 20, 5 << 20),
        name="weight_sum",
    )(place, mine, below, above)


def weight_call(kernel, name, parts, outs, extra, place, grad, *more):
    return pl.pallas_call(
        kernel,
        in_specs=[SMEM_SPEC, ANY_SPEC] + [VMEM_SPEC] * len(more),
        out_specs=[VMEM_SPEC] * len(outs),
        out_shape=outs,
        scratch_shapes=[pltpu.VMEM((ROWS, QUARTER), BF), pltpu.SemaphoreType.DMA] + extra,
        compiler_params=PLAIN,
        cost_estimate=cost(parts * 2 * ROWS * QUARTER * W, parts * 3 << 20),
        name=name,
    )(place, grad, *more)


CHUNK = 256


def backward_block(keys, values, queries, grads, log_total, row_dot):
    scores = nt(keys, queries)
    probs = jnp.exp2(scores * SCALE2 - log_total)
    grad_probs = nt(values, grads)
    grad_scores = (probs * (grad_probs - row_dot)).astype(BF)
    grad_values = nn(probs.astype(BF), grads)
    grad_keys = nn(grad_scores, queries) * SCALE
    grad_queries_t = nn(keys.T, grad_scores)
    return grad_keys, grad_values, grad_queries_t


def backward_common(qa, qb, da, db, fin):
    queries = jnp.concatenate([flat(qa), flat(qb)], axis=0)
    grads = jnp.concatenate([da[...], db[...]], axis=0)
    return queries, grads, fin[0, 0:1], fin[0, 1:2]


def chunks_of(x):
    return [x[i * CHUNK : (i + 1) * CHUNK] for i in range(ROWS // CHUNK)]


def run_block(keys, values, common):
    dks, dvs, dqt = [], [], None
    for k, v in zip(chunks_of(keys), chunks_of(values)):
        dk, dv, q = backward_block(k, v, *common)
        dks.append(dk)
        dvs.append(dv)
        dqt = q if dqt is None else dqt + q
    return jnp.concatenate(dks, axis=0), jnp.concatenate(dvs, axis=0), dqt


def store_halves(low, high, i, x):
    low[:, i] = x[: ROWS // 2].astype(low.dtype).reshape(U // 2, T, HD)
    high[:, i] = x[ROWS // 2 :].astype(high.dtype).reshape(U // 2, T, HD)


def far_kernel(qa, qb, da, db, fin, kv3, low_ref, high_ref, dqt_ref):
    common = backward_common(qa, qb, da, db, fin)
    dk, dv, dqt = run_block(kv3[:, 0].reshape(ROWS, HD), kv3[:, 1].reshape(ROWS, HD), common)
    store_halves(low_ref, high_ref, 0, dk)
    store_halves(low_ref, high_ref, 1, dv)
    dqt_ref[...] = dqt


def store_sum(o, i, x, got, first):
    half = ROWS // 2
    at = slice(first, first + half)
    rest = slice(half - first, ROWS - first)
    u, r = slice(first // T, (first + half) // T), slice((half - first) // T, (ROWS - first) // T)
    o[u, i] = (x[at] + got[:, i].reshape(half, HD).astype(F32)).astype(BF).reshape(U // 2, T, HD)
    o[r, i] = x[rest].astype(BF).reshape(U // 2, T, HD)


def near_kernel(qa, qb, da, db, fin, kv1, kv2, dqt_in, low, high, o1_ref, o2_ref, dqt_ref):
    common = backward_common(qa, qb, da, db, fin)
    total = dqt_in[...]
    for kv, o, got, first in ((kv1, o1_ref, high, ROWS // 2), (kv2, o2_ref, low, 0)):
        dk, dv, dqt = run_block(kv[:, 0].reshape(ROWS, HD), kv[:, 1].reshape(ROWS, HD), common)
        store_sum(o, 0, dk, got, first)
        store_sum(o, 1, dv, got, first)
        total = total + dqt
    dqt_ref[...] = total


def own_kernel(qa, qb, da, db, fin, kv0, dqt_in, o0_ref, qkeep_ref, qsend_ref):
    common = backward_common(qa, qb, da, db, fin)
    dk, dv, dqt = run_block(kv0[:, 0].reshape(ROWS, HD), kv0[:, 1].reshape(ROWS, HD), common)
    o0_ref[:, 0] = dk.reshape(U, T, HD)
    o0_ref[:, 1] = dv.reshape(U, T, HD)
    total = (dqt_in[...] + dqt) * SCALE
    qkeep_ref[...] = total[:, :ROWS].T.reshape(U, T, HD)
    qsend_ref[...] = total[:, ROWS:].T.astype(BF).reshape(U, T, HD)


COMMON_SPECS = [Q_SPEC, Q_SPEC, ROW_SPEC, ROW_SPEC, ST_SPEC]


def backward_far(common, kv3):
    return pl.pallas_call(
        far_kernel,
        grid=(HEADS,),
        in_specs=COMMON_SPECS + [KV_SPEC],
        out_specs=[HALF_SPEC, HALF_SPEC, OT_SPEC],
        out_shape=[struct((U // 2, 2, T, W), BF)] * 2 + [struct((W, 2 * ROWS), F32)],
        compiler_params=PARAMS,
        cost_estimate=cost(5 * 2 * 1024 * 512 * W, 6 << 20),
        name="backward_far",
    )(*common, kv3)


def backward_near(common, kv1, kv2, dqt, low, high):
    return pl.pallas_call(
        near_kernel,
        grid=(HEADS,),
        in_specs=COMMON_SPECS + [KV_SPEC, KV_SPEC, OT_SPEC, HALF_SPEC, HALF_SPEC],
        out_specs=[KV_SPEC, KV_SPEC, OT_SPEC],
        out_shape=[struct((U, 2, T, W), BF)] * 2 + [struct((W, 2 * ROWS), F32)],
        compiler_params=PARAMS,
        cost_estimate=cost(5 * 2 * 1024 * 1024 * W, 9 << 20),
        name="backward_near",
    )(*common, kv1, kv2, dqt, low, high)


def backward_own(common, kv0, dqt):
    return pl.pallas_call(
        own_kernel,
        grid=(HEADS,),
        in_specs=COMMON_SPECS + [KV_SPEC, OT_SPEC],
        out_specs=[KV_SPEC, Q_SPEC, Q_SPEC],
        out_shape=[struct((U, 2, T, W), F32), struct((U, T, W), F32), struct((U, T, W), BF)],
        compiler_params=PARAMS,
        cost_estimate=cost(5 * 2 * 1024 * 512 * W, 8 << 20),
        name="backward_own",
    )(*common, kv0, dqt)


def move(x, axis, to, n):
    return lax.ppermute(x, axis, [(i, to(i)) for i in range(n)])


def y_shift(x, d):
    return move(x, "blk", lambda i: i // 4 * 4 + (i + d) % 4, 8)


def z_shift(x, d):
    return move(x, ("dp", "blk"), lambda i: (i // 4 + d) % 4 * 4 + i % 4, 16)


def z_swap(x):
    return move(x, "blk", lambda i: (i + 4) % 8, 8)


def by_head(*rows):
    stacked = jnp.concatenate([r.reshape(T, U, 1, W) for r in rows], axis=2)
    return jnp.transpose(stacked, (1, 2, 0, 3))


def exchange(x):
    return lax.all_to_all(x, "uly", split_axis=0, concat_axis=0, tiled=True)


def to_tokens(x):
    got = exchange(x)
    return [jnp.transpose(got[:, i], (1, 0, 2)).reshape(T, U * W) for i in range(x.shape[1])]


def after(x, *others):
    return lax.optimization_barrier((x, *others))[0]


def per_device(query_rows, key_rows, value_rows, out_grad, out_weight):
    uly, blk = lax.axis_index("uly"), lax.axis_index("blk")
    place = jnp.stack([uly // 2, uly % 2, lax.axis_index("dp") * 2 + blk // 4, blk % 4]).astype(jnp.int32)
    leaving = by_head(key_rows, value_rows, query_rows)
    grad_block = lax.all_gather(out_grad, "uly", axis=0, tiled=True)
    shards = (out_weight, y_shift(out_weight, -1), y_shift(out_weight, 2), y_shift(out_weight, 1))
    heads = exchange(leaving)
    shards, place = after((shards, place), leaving)
    weight_own = stacked_rows(*shards)
    heads = after(heads, weight_own)
    kv0, qa = heads[:, :2], heads[:, 2]
    kv_prev, kv_next = y_shift(kv0, 1), y_shift(kv0, -1)
    qb = z_swap(qa)
    weight_below, weight_above = z_shift(weight_own, 1), z_shift(weight_own, -1)
    cut = QUARTER // 2
    weights = (weight_own, weight_above, z_shift(weight_above[:cut], -1), z_shift(weight_below[cut:], 1), weight_below)
    kv_far = y_shift(kv_prev, 1)
    ot, st = forward_near(qa, qb, kv0, kv_prev, kv_next)
    da = project(after(place, ot), grad_block, weights)
    db = z_swap(da)
    ot, st = forward_far(after(qa, da), qb, kv_far, ot, st)
    st = row_dots(ot, st, da, db)
    o_keep, o_send, fin = merge(ot, st, z_swap(st))
    attn_out = (o_keep + z_swap(o_send).astype(F32)).astype(BF)
    common = (qa, qb, da, db, fin)

    low, high, dqt = backward_far(common, kv_far)
    low_got, high_got = y_shift(low, 1), y_shift(high, -1)
    half = struct((QUARTER // 2, W), BF)
    a, b = weight_call(weight_far_kernel, "weight_far", 1, [half, half], [], place, grad_block, after(attn_out, dqt))
    a_got, b_got = z_shift(a, 1), z_shift(b, -1)
    to_prev, to_next, dqt = backward_near(common, kv_prev, kv_next, after(dqt, a, b), low_got, high_got)
    from_below, from_above = y_shift(to_next, 1), y_shift(to_prev, -1)
    g_own, q_keep, q_send = backward_own(common, kv0, dqt)
    whole = struct((QUARTER, W), BF)
    up, down = weight_call(
        weight_near_kernel, "weight_near", 2, [whole, whole], [], place, grad_block, after(attn_out, q_send), a_got, b_got
    )
    below, above = z_shift(up, 1), z_shift(down, -1)
    dq = (after(q_keep, up) + z_swap(q_send).astype(F32)).astype(BF)
    dkv = (g_own + from_below.astype(F32) + from_above.astype(F32)).astype(BF)
    grads = jnp.concatenate([dkv, dq[:, None]], axis=1)
    grad_key, grad_value, grad_query = to_tokens(grads)
    outs = [struct((QUARTER, W), F32)]
    (mine,) = weight_call(weight_own_kernel, "weight_own", 1, outs, [], place, grad_block, after(attn_out, grads))
    o0, o1, o2, o3 = weight_sum(place, mine, below, above)
    grad_weight = o0 + y_shift(o1, 1).astype(F32) + y_shift(o2, 2).astype(F32) + y_shift(o3, -1).astype(F32)
    return (grad_query, grad_key, grad_value, grad_weight)


def solution(mesh):
    rows = P(("dp", "blk", "uly"), None)
    weight = P(("dp", "blk"), "uly")
    return jax.shard_map(
        per_device,
        mesh=mesh,
        in_specs=(rows, rows, rows, rows, weight),
        out_specs=(rows, rows, rows, weight),
        check_vma=False,
    )
```
